32 devices in a mesh: rep: 4 (over y, x), blk: 8 (over z, core).
Axes of the slice: x: 2, y: 2, z: 4, core: 2. Of those that a mesh axis runs over, the one named last changes fastest.
Arguments:
- feats: bfloat16 [128, 128, 256], P('blk'), may hold values from -6 to 6
- requests: int32 [8, 8], P('blk'), may hold values from 0 to 15
- tile_dest: int32 [8, 64], P('blk'), may hold values from 0 to 15, as said below
- tile_slot: int32 [8, 64], P('blk'), may hold values from 0 to 7, as said below
- tile_vals: bfloat16 [8, 64, 128, 128], P('blk', None, 'rep'), may hold values from -0.25 to 0.25
- w_self: bfloat16 [256, 256], replicated, may hold values from -0.375 to 0.375
- w_neigh: bfloat16 [256, 256], replicated, may hold values from -0.375 to 0.375
- bias: float32 [256], replicated, may hold values from -3 to 3
- cotangent: bfloat16 [128, 128, 256], P('blk', 'rep'), may hold values from -6 to 6
Outputs:
- hidden: bfloat16 [128, 128, 256], P('blk', 'rep')
- grad_self: float32 [256, 256], replicated
- grad_neigh: float32 [256, 256], replicated
- grad_bias: float32 [256], replicated
- feat_grad: bfloat16 [128, 128, 256], P('blk', 'rep')
The draws below stay inside these ranges and needn't reach their ends.
Inputs may be any that keep to these rules, and one draw needn't show every extreme that they name: `tile_slot`: for each reader b, every owner index is named by exactly 8 of its tiles. `tile_dest`: no two tiles of one reader have both the same destination block and the same owner.
All inputs are finite; a program needn't handle non-finite values.
Results may differ from the reference program's by a relative error of at most 0.015.
Values may be sent and summed in bfloat16 or wider, within the bound.
No kernel may reach another device: no remote copies, remote signals or barrier semaphores. Data moves between devices by JAX's collectives and lax.ppermute only.
A program may use at most 128 MiB of HBM per device.

```python
import math
import jax
import jax.numpy as jnp
from jax import lax

D = 256
TILE = 128
BLK_DEV = 16
OWNERS = 8
TILES = 64
NBLOCKS = 128
NODES = 16384


def tile_pairs(key):
    base = jax.random.fold_in(key, 7)

    def one_reader(reader):
        reader_key = jax.random.fold_in(base, reader)
        order = jax.random.permutation(jax.random.fold_in(reader_key, 1), TILES)
        owner_ids = order % OWNERS
        ranking = order // OWNERS

        def one_owner(owner):
            return jax.random.permutation(jax.random.fold_in(reader_key, owner + 2), BLK_DEV)
        tables = jax.vmap(one_owner)(jnp.arange(OWNERS))
        dest_ids = tables[owner_ids, ranking]
        return (owner_ids.astype(jnp.int32), dest_ids.astype(jnp.int32))
    return jax.vmap(one_reader)(jnp.arange(OWNERS))


def draw_tile_slot(key, part):
    return tile_pairs(key)[0]


def draw_tile_dest(key, part):
    return tile_pairs(key)[1]


def set_ends(drawn, key, low, top_value):
    spot = [jax.random.randint(jax.random.fold_in(key, axis), (), 0, length) for axis, length in enumerate(drawn.shape)]
    widest = drawn.shape.index(max(drawn.shape))
    neighbour = spot[:widest] + [(spot[widest] + 1) % drawn.shape[widest]] + spot[widest + 1:]
    return drawn.at[tuple(spot)].set(low).at[tuple(neighbour)].set(top_value)


def block_scale(key, extent, shards, smallest, largest):
    def one(dim, blocks):
        draws = jax.random.uniform(jax.random.fold_in(jax.random.fold_in(key, 6), dim), (blocks,), jnp.float32, smallest / len(shards), largest / len(shards))
        return jnp.repeat(jnp.exp(draws), extent[dim] // blocks).reshape((-1,) + (1,) * (len(extent) - dim - 1))

    loudness = one(*shards[0])
    for cut in shards[1:]:
        loudness = loudness * one(*cut)
    return loudness


def noise(stream_key, extent, scale, limit, pieces=(), held_as=jnp.bfloat16):
    array = jax.random.normal(stream_key, extent, jnp.float32) * scale
    if len(pieces) > 0:
        array = block_scale(stream_key, extent, pieces, -0.22, 0.18) * array
    return jnp.clip(array, min=-limit, max=limit).astype(held_as)


def setup_inputs(seed: int = 0) -> dict:
    key_of = jax.random.split(jax.random.key(seed), 10)
    feats = noise(key_of[0], (NBLOCKS, TILE, D), 1.0, 6.0, ((0, 8),))
    requests = set_ends(jax.random.randint(key_of[1], (OWNERS, OWNERS), 0, BLK_DEV), jax.random.fold_in(key_of[1], 1), 0, BLK_DEV - 1).astype(jnp.int32)
    tile_dest = draw_tile_dest(jax.random.fold_in(key_of[9], 71), 0)
    tile_slot = draw_tile_slot(jax.random.fold_in(key_of[9], 71), 0)
    tile_vals = noise(key_of[4], (OWNERS, TILES, TILE, TILE), (OWNERS * TILE // 2) ** -0.5, 0.25, ((0, 8), (2, 4)))
    w_self = noise(key_of[5], (D, D), D ** -0.5, 0.375)
    w_neigh = noise(key_of[6], (D, D), D ** -0.5, 0.375)
    bias = noise(key_of[7], (D,), 0.5, 3.0, (), jnp.float32)
    cotangent = noise(key_of[8], (NBLOCKS, TILE, D), 1.0, 6.0, ((0, 8), (1, 4)))
    return {"feats": feats, "requests": requests, "tile_dest": tile_dest, "tile_slot": tile_slot, "tile_vals": tile_vals, "w_self": w_self, "w_neigh": w_neigh, "bias": bias, "cotangent": cotangent}


def source_blocks(requests, tile_slot, reader):
    owner_ids = tile_slot[reader]
    return (owner_ids * BLK_DEV + requests[owner_ids, reader]).astype(jnp.int32)

def reference(feats, requests, tile_dest, tile_slot, tile_vals, w_self, w_neigh, bias, cotangent):

    def forward_one(reader):
        source_ids = source_blocks(requests, tile_slot, reader)
        sources = feats[source_ids].astype(jnp.float32)
        products = jnp.einsum('tij,tjd->tid', tile_vals[reader].astype(jnp.float32), sources)
        return jax.ops.segment_sum(products, tile_dest[reader], num_segments=BLK_DEV)
    readers = jnp.arange(OWNERS, dtype=jnp.int32)
    aggregate = lax.map(forward_one, readers)
    aggregate = aggregate.reshape(NODES, D).astype(jnp.bfloat16)
    feat_rows = feats.reshape(NODES, D)
    preact = jnp.dot(feat_rows, w_self, preferred_element_type=jnp.float32)
    preact = preact + jnp.dot(aggregate, w_neigh, preferred_element_type=jnp.float32) + bias
    hidden = jax.nn.silu(preact).astype(jnp.bfloat16)
    gating = jax.nn.sigmoid(preact)
    grad_pre = (cotangent.reshape(NODES, D).astype(jnp.float32) * gating * (1.0 + preact * (1.0 - gating))).astype(jnp.bfloat16)
    grad_scale = 1.0 / math.sqrt(NODES)
    grad_self = jnp.dot(feat_rows.T, grad_pre, preferred_element_type=jnp.float32) * grad_scale
    grad_neigh = jnp.dot(aggregate.T, grad_pre, preferred_element_type=jnp.float32) * grad_scale
    grad_bias = lax.optimization_barrier(jnp.sum(grad_pre.astype(jnp.float32), axis=0)) * grad_scale
    back_rows = jnp.dot(grad_pre, w_neigh.T, preferred_element_type=jnp.float32).astype(jnp.bfloat16)
    back_rows = back_rows.reshape(NBLOCKS, TILE, D)

    def backward_one(total, reader):
        source_ids = source_blocks(requests, tile_slot, reader)
        local_back = lax.dynamic_slice_in_dim(back_rows, reader * BLK_DEV, BLK_DEV, 0)
        selected = local_back[tile_dest[reader]].astype(jnp.float32)
        products = jnp.einsum('tij,tid->tjd', tile_vals[reader].astype(jnp.float32), selected)
        return (total.at[source_ids].add(products), None)
    total, _ = lax.scan(backward_one, jnp.zeros((NBLOCKS, TILE, D), jnp.float32), readers)
    self_term = jnp.dot(grad_pre, w_self.T, preferred_element_type=jnp.float32)
    feat_grad = (self_term + total.reshape(NODES, D)).astype(jnp.bfloat16).reshape(NBLOCKS, TILE, D)
    return (hidden.reshape(NBLOCKS, TILE, D), grad_self, grad_neigh, grad_bias, feat_grad)
```

```python
import math

import jax
import jax.numpy as jnp
from jax import lax
from jax.experimental import pallas as pl
from jax.experimental.pallas import tpu as pltpu
from jax.sharding import PartitionSpec as P

BF16 = jnp.bfloat16
F32 = jnp.float32
PAD = 16
LIMIT = 56 * 1024 * 1024
NT = (((1,), (1,)), ((), ()))

VMEM = pl.BlockSpec(memory_space=pltpu.VMEM)
SMEM = pl.BlockSpec(memory_space=pltpu.SMEM)
ANY = pl.BlockSpec(memory_space=pl.ANY)


def call(body, in_specs, out_shape, out_specs, scratch=(), name=None, flops=0, bytes_accessed=0):
    return pl.pallas_call(
        body,
        in_specs=in_specs,
        out_shape=out_shape,
        out_specs=out_specs,
        scratch_shapes=scratch,
        name=name,
        cost_estimate=pl.CostEstimate(
            flops=flops, bytes_accessed=bytes_accessed, transcendentals=0
        ),
        compiler_params=pltpu.CompilerParams(vmem_limit_bytes=LIMIT),
    )


def struct(shape, dtype):
    return jax.ShapeDtypeStruct(shape, dtype)


def aligned(index, size):
    return pl.ds(pl.multiple_of(index * size, size), size)


def dot(a, b):
    return jnp.dot(a, b, preferred_element_type=F32)


def butterfly_sum(terms):
    while len(terms) > 1:
        terms = [terms[i] + terms[i + 1] for i in range(0, len(terms), 2)]
    return terms[0]


def split_rows(row):
    high = row.astype(BF16)
    low = (row - high.astype(F32)).astype(BF16)
    place = lax.broadcasted_iota(jnp.int32, (PAD, row.shape[1]), 0)
    spread = jnp.where(place == 0, high.astype(F32), 0.0)
    spread = jnp.where(place == 1, low.astype(F32), spread)
    return spread.astype(BF16)


def join_rows(rows):
    return jnp.sum(rows.astype(F32), axis=0, keepdims=True)


def swap(array, axis, size, distance):
    return lax.ppermute(array, axis, [(i, i ^ distance) for i in range(size)])


def prepare_kernel(
    dest, slot, tiles, feats, w_self, bias, dense, dense_t, rows_t, pre_self, rows, sem
):
    tile_count, quarter, width = tiles.shape[1:]
    owners = dense.shape[1] // width
    rep = lax.axis_index("rep")
    copy = pltpu.make_async_copy(feats.at[:, aligned(rep, quarter), :], rows, sem)
    copy.start()
    dense[...] = jnp.zeros_like(dense)

    def place(t, carry):
        dense[aligned(dest[0, t], quarter), aligned(slot[0, t], width)] = tiles[0, t]
        return carry

    lax.fori_loop(0, tile_count, place, 0)

    def turn(o, carry):
        dense_t[aligned(o, width), :] = dense[:, aligned(o, width)].T
        return carry

    lax.fori_loop(0, owners, turn, 0)
    copy.wait()
    own = rows[...].reshape(rows.shape[0] * quarter, rows.shape[2])
    rows_t[...] = own.T
    pre_self[...] = dot(own, w_self[...]) + bias[...]


def layer_kernel(
    grad_scale, owners, dense, dense_t, sources, rows_t, pre_self, cotangent, w_self, w_neigh,
    hidden, self_term, *rest
):
    messages, contributions, gradients = rest[:-2], rest[-2], rest[-1]
    replicas = len(messages)
    features = w_self.shape[0]
    width = contributions.shape[1]
    quarter = width // replicas
    share = features // replicas
    zs = owners // 2
    rep = lax.axis_index("rep")
    agg = dot(dense[...], sources[...]).astype(BF16)
    preact = pre_self[...] + dot(agg, w_neigh[...])
    gating = jax.nn.sigmoid(preact)
    hidden[...] = (preact * gating).astype(BF16).reshape(hidden.shape)
    grads = cotangent[...].reshape(preact.shape).astype(F32)
    grad_pre = (grads * gating * (1.0 + preact * (1.0 - gating))).astype(BF16)
    back = lax.dot_general(grad_pre, w_neigh[...], NT, preferred_element_type=F32).astype(BF16)

    def contribute(o, carry):
        contributions[o] = dot(dense_t[aligned(o, width), :], back).astype(BF16)
        return carry

    lax.fori_loop(0, owners, contribute, 0, unroll=owners <= 8)
    gradients[0] = (dot(rows_t[...], grad_pre) * grad_scale).astype(BF16)
    gradients[1] = (dot(agg.T, grad_pre) * grad_scale).astype(BF16)
    bias_rows = split_rows(
        jnp.sum(grad_pre.astype(F32), axis=0, keepdims=True) * grad_scale
    )
    base = owners * quarter
    for k, message in enumerate(messages):
        target = rep ^ k
        for core in range(2):
            for z in range(zs):
                start = (core * zs + z) * quarter
                message[start : start + quarter] = contributions[
                    2 * z + core, aligned(target, quarter), :
                ]
        for half in range(2):
            start = base + half * share
            message[start : start + share] = gradients[half, aligned(target, share), :]
        message[base + 2 * share :] = bias_rows
    self_term[...] = lax.dot_general(grad_pre, w_self[...], NT, preferred_element_type=F32)


def rep_sum_kernel(share, *refs):
    arrived, keep, send = refs[:-2], refs[-2], refs[-1]
    core = lax.axis_index("blk") % 2
    rows = keep.shape[0] - PAD - share
    base = 2 * rows
    bias_rows = split_rows(butterfly_sum([join_rows(a[base + 2 * share :]) for a in arrived]))
    for out, side in ((keep, core), (send, 1 - core)):
        total = sum(a[aligned(side, rows), :].astype(F32) for a in arrived)
        out[:rows] = total.astype(BF16)
        place = pl.ds(pl.multiple_of(base + side * share, PAD), share)
        total = sum(a[place, :].astype(F32) for a in arrived)
        out[rows : rows + share] = total.astype(BF16)
        out[rows + share :] = bias_rows


def core_join_kernel(share, keep, got, *messages):
    zs = len(messages)
    z = lax.axis_index("blk") // 2
    rows = keep.shape[0] - PAD - share
    quarter = rows // zs
    grads = keep[rows : rows + share].astype(F32) + got[rows : rows + share].astype(F32)
    grads = grads.astype(BF16)
    bias_rows = split_rows(join_rows(keep[rows + share :]) + join_rows(got[rows + share :]))
    for k, message in enumerate(messages):
        place = aligned(z ^ k, quarter)
        message[:quarter] = keep[place, :]
        message[quarter : 2 * quarter] = got[place, :]
        message[2 * quarter : 2 * quarter + share] = grads
        message[2 * quarter + share :] = bias_rows


def finish_kernel(share, requests, self_term, *refs):
    arrived, (feat_grad, piece, grad_bias, total) = refs[:-4], refs[-4:]
    quarter = total.shape[1]
    blk = lax.axis_index("blk")
    base = 2 * quarter
    piece[...] = butterfly_sum([a[base : base + share].astype(F32) for a in arrived]).astype(BF16)
    bias_sum = butterfly_sum([join_rows(a[base + share :]) for a in arrived])
    grad_bias[...] = bias_sum
    total[...] = self_term[...].reshape(total.shape)
    for k, message in enumerate(arrived):
        for other in range(2):
            block = requests[0, blk ^ (2 * k + other)]
            total[block] += message[other * quarter : (other + 1) * quarter].astype(F32)
    feat_grad[...] = total[...].astype(BF16)


def gather_kernel(*refs):
    pieces, out = refs[:-1], refs[-1]
    share = pieces[0].shape[0]
    rep = lax.axis_index("rep")
    for k, piece in enumerate(pieces):
        out[aligned(rep ^ k, share), :] = piece[...]


def widen_kernel(mine, other, grad_self, grad_neigh):
    core = lax.axis_index("blk") % 2
    first = core == 0
    a = mine[...].astype(F32)
    b = other[...].astype(F32)
    grad_self[...] = jnp.where(first, a, b)
    grad_neigh[...] = jnp.where(first, b, a)


def on_device(feats, requests, tile_dest, tile_slot, tile_vals, w_self, w_neigh, bias, cotangent):
    owners = lax.axis_size("blk")
    replicas = lax.axis_size("rep")
    zs = owners // 2
    blk_dev, width, features = feats.shape
    quarter = width // replicas
    row_count = blk_dev * quarter
    share = features // replicas
    grad_scale = 1.0 / math.sqrt(owners * blk_dev * width)

    outgoing = feats.at[requests[0]].get(mode="promise_in_bounds")
    sources = lax.all_to_all(outgoing, "blk", split_axis=0, concat_axis=0, tiled=True)
    dense, dense_t, rows_t, pre_self = call(
        prepare_kernel,
        [SMEM, SMEM, VMEM, ANY, VMEM, VMEM],
        (
            struct((row_count, owners * width), BF16),
            struct((owners * width, row_count), BF16),
            struct((features, row_count), BF16),
            struct((row_count, features), F32),
        ),
        (VMEM,) * 4,
        (pltpu.VMEM((blk_dev, quarter, features), BF16), pltpu.SemaphoreType.DMA),
        name="prepare",
        flops=2 * row_count * features * features,
        bytes_accessed=4 * 1024 * 1024,
    )(tile_dest, tile_slot, tile_vals, feats, w_self, bias.reshape(1, features))

    message_rows = owners * quarter + 2 * share + PAD
    outs = call(
        lambda *refs: layer_kernel(grad_scale, owners, *refs),
        [VMEM] * 8,
        (
            struct((blk_dev, quarter, features), BF16),
            struct((row_count, features), F32),
        )
        + (struct((message_rows, features), BF16),) * replicas,
        (VMEM,) * (2 + replicas),
        (
            pltpu.VMEM((owners, width, features), BF16),
            pltpu.VMEM((2, features, features), BF16),
        ),
        name="layer",
        flops=4 * row_count * features * owners * width,
        bytes_accessed=6 * 1024 * 1024,
    )(
        dense, dense_t, sources.reshape(owners * width, features), rows_t, pre_self, cotangent,
        w_self, w_neigh,
    )
    hidden, self_term, messages = outs[0], outs[1], outs[2:]
    arrived = [messages[0]] + [
        swap(messages[k], "rep", replicas, k) for k in range(1, replicas)
    ]
    half = struct((zs * quarter + share + PAD, features), BF16)
    keep, send = call(
        lambda *refs: rep_sum_kernel(share, *refs),
        [VMEM] * replicas,
        (half, half),
        (VMEM, VMEM),
        name="rep_sum",
        bytes_accessed=1024 * 1024,
    )(*arrived)
    got = swap(send, "blk", owners, 1)
    parcels = call(
        lambda *refs: core_join_kernel(share, *refs),
        [VMEM, VMEM],
        (struct((2 * quarter + share + PAD, features), BF16),) * zs,
        (VMEM,) * zs,
        name="core_join",
        bytes_accessed=512 * 1024,
    )(keep, got)
    landed = [parcels[0]] + [swap(parcels[k], "blk", owners, 2 * k) for k in range(1, zs)]
    feat_grad, piece, grad_bias = call(
        lambda *refs: finish_kernel(share, *refs),
        [SMEM, VMEM] + [VMEM] * zs,
        (
            struct((blk_dev, quarter, features), BF16),
            struct((share, features), BF16),
            struct((1, features), F32),
        ),
        (VMEM,) * 3,
        (pltpu.VMEM((blk_dev, quarter, features), F32),),
        name="finish",
        bytes_accessed=1024 * 1024,
    )(requests, self_term, *landed)
    pieces = [piece] + [swap(piece, "rep", replicas, k) for k in range(1, replicas)]
    whole = struct((features, features), F32)
    mine = call(
        gather_kernel,
        [VMEM] * replicas,
        struct((features, features), BF16),
        VMEM,
        name="gather_pieces",
    )(*pieces)
    other = swap(mine, "blk", owners, 1)
    grad_self, grad_neigh = call(
        widen_kernel, [VMEM, VMEM], (whole, whole), (VMEM, VMEM), name="widen"
    )(mine, other)
    return (hidden, grad_self, grad_neigh, grad_bias.reshape(features), feat_grad)


def solution(mesh):
    in_specs = (
        P("blk", None, None),
        P("blk", None),
        P("blk", None),
        P("blk", None),
        P("blk", None, "rep", None),
        P(),
        P(),
        P(),
        P("blk", "rep", None),
    )
    out_specs = (P("blk", "rep", None), P(), P(), P(), P("blk", "rep", None))
    return jax.shard_map(
        on_device, mesh=mesh, in_specs=in_specs, out_specs=out_specs, check_vma=False
    )
```

```python
import math

import jax
import jax.numpy as jnp
from jax import lax
from jax.experimental import pallas as pl
from jax.experimental.pallas import tpu as pltpu
from jax.sharding import PartitionSpec as P

BF16 = jnp.bfloat16
F32 = jnp.float32
PAD = 16
MIB = 1024 * 1024
NT = (((1,), (1,)), ((), ()))

VMEM = pl.BlockSpec(memory_space=pltpu.VMEM)
SMEM = pl.BlockSpec(memory_space=pltpu.SMEM)
HBM = pl.BlockSpec(memory_space=pltpu.HBM)


def size_of(array):
    return math.prod(array.shape) * jnp.dtype(array.dtype).itemsize


def call(body, in_specs, out_shape, out_specs, scratch=(), name=None, flops=0, limit=0):
    def run(*operands):
        moved = sum(size_of(a) for a in jax.tree.leaves((operands, out_shape)))
        return pl.pallas_call(
            body,
            in_specs=in_specs,
            out_shape=out_shape,
            out_specs=out_specs,
            scratch_shapes=scratch,
            name=name,
            cost_estimate=pl.CostEstimate(
                flops=flops, bytes_accessed=moved, transcendentals=0
            ),
            compiler_params=pltpu.CompilerParams(
                vmem_limit_bytes=limit or min(moved + moved // 4 + 2 * MIB, 56 * MIB)
            ),
        )(*operands)

    return run


def struct(shape, dtype):
    return jax.ShapeDtypeStruct(shape, dtype)


def aligned(index, size):
    return pl.ds(pl.multiple_of(index * size, size), size)


def dot(a, b):
    return jnp.dot(a, b, preferred_element_type=F32)


def butterfly_sum(terms):
    while len(terms) > 1:
        terms = [terms[i] + terms[i + 1] for i in range(0, len(terms), 2)]
    return terms[0]


def split_rows(row):
    high = row.astype(BF16)
    low = (row - high.astype(F32)).astype(BF16)
    place = lax.broadcasted_iota(jnp.int32, (PAD, row.shape[1]), 0)
    spread = jnp.where(place == 0, high.astype(F32), 0.0)
    spread = jnp.where(place == 1, low.astype(F32), spread)
    return spread.astype(BF16)


def join_rows(rows):
    return jnp.sum(rows.astype(F32), axis=0, keepdims=True)


def swap(array, axis, size, distance):
    return lax.ppermute(array, axis, [(i, i ^ distance) for i in range(size)])


def pick_kernel(requests_in, feats, out, requests, sems):
    pltpu.sync_copy(requests_in, requests)
    copies = [
        pltpu.make_async_copy(feats.at[requests[0, reader]], out.at[reader], sems.at[reader])
        for reader in range(out.shape[0])
    ]
    for copy in copies:
        copy.start()
    for copy in copies:
        copy.wait()


def prepare_kernel(
    owners, dest, slot, tiles, feats, w_self, w_neigh, cotangent, packed, rows, sem
):
    tile_count, quarter, width = tiles.shape[1:]
    row_count = packed.shape[1]
    features = w_self.shape[0]
    per_slab = row_count // width
    slabs = owners // per_slab
    rep = lax.axis_index("rep")
    copy = pltpu.make_async_copy(feats.at[:, aligned(rep, quarter), :], rows, sem)
    copy.start()
    packed[:slabs] = jnp.zeros((slabs, row_count, row_count), packed.dtype)

    def place(t, carry):
        owner = slot[0, t]
        packed[
            owner // per_slab, aligned(dest[0, t], quarter), aligned(owner % per_slab, width)
        ] = tiles[0, t]
        return carry

    lax.fori_loop(0, tile_count, place, 0)

    def turn(slab, carry):
        packed[slabs + slab] = packed[slab].T
        return carry

    lax.fori_loop(0, slabs, turn, 0)
    copy.wait()
    own = rows[...].reshape(row_count, features)
    packed[2 * slabs, :, :features] = own
    packed[2 * slabs, :, features:] = cotangent[...].reshape(row_count, features)
    packed[2 * slabs + 1, :features] = own.T
    packed[2 * slabs + 1, features:, :features] = w_self[...]
    packed[2 * slabs + 1, features:, features:] = w_neigh[...]


def layer_kernel(grad_scale, owners, replicas, sources, packed, bias, *refs):
    preact_out, grad_pre_out, messages = refs[0], refs[1], refs[2 : 2 + replicas]
    contributions, gradients = refs[2 + replicas :]
    row_count, features = preact_out.shape
    width = contributions.shape[1]
    quarter = width // replicas
    share = features // replicas
    per_slab = row_count // width
    slabs = owners // per_slab
    zs = owners // 2
    rep = lax.axis_index("rep")
    rows = packed[2 * slabs, :, :features]
    cotangent = packed[2 * slabs, :, features:]
    rows_t = packed[2 * slabs + 1, :features]
    w_self = packed[2 * slabs + 1, features:, :features]
    w_neigh = packed[2 * slabs + 1, features:, features:]
    agg = dot(packed[0], sources[:row_count])
    if slabs <= 4:
        for slab in range(1, slabs):
            agg += dot(packed[slab], sources[slab * row_count : (slab + 1) * row_count])
    else:
        agg = lax.fori_loop(
            1, slabs, lambda i, a: a + dot(packed[i], sources[aligned(i, row_count), :]), agg
        )
    agg = agg.astype(BF16)
    preact = dot(rows, w_self) + dot(agg, w_neigh) + bias[...]
    preact_out[...] = preact
    gating = jax.nn.sigmoid(preact)
    grad_pre = (
        cotangent.astype(F32) * gating * (1.0 + preact * (1.0 - gating))
    ).astype(BF16)
    grad_pre_out[...] = grad_pre
    back = lax.dot_general(grad_pre, w_neigh, NT, preferred_element_type=F32).astype(BF16)

    def contribute(slab, carry):
        contributions[pl.ds(slab * per_slab, per_slab)] = (
            dot(packed[slabs + slab], back).astype(BF16).reshape(per_slab, width, features)
        )
        return carry

    lax.fori_loop(0, slabs, contribute, 0, unroll=slabs <= 4)
    gradients[0] = (dot(rows_t, grad_pre) * grad_scale).astype(BF16)
    gradients[1] = (dot(agg.T, grad_pre) * grad_scale).astype(BF16)
    bias_rows = split_rows(
        jnp.sum(grad_pre.astype(F32), axis=0, keepdims=True) * grad_scale
    )
    base = owners * quarter
    for k, message in enumerate(messages):
        target = rep ^ k
        for core in range(2):
            for z in range(zs):
                start = (core * zs + z) * quarter
                message[start : start + quarter] = contributions[
                    2 * z + core, aligned(target, quarter), :
                ]
        for half in range(2):
            start = base + half * share
            message[start : start + share] = gradients[half, aligned(target, share), :]
        message[base + 2 * share :] = bias_rows


def own_kernel(preact, grad_pre, w_self, hidden, self_term):
    value = preact[...]
    hidden[...] = (value * jax.nn.sigmoid(value)).astype(BF16).reshape(hidden.shape)
    self_term[...] = lax.dot_general(grad_pre[...], w_self[...], NT, preferred_element_type=F32)


def rep_sum_kernel(share, *refs):
    arrived, keep, send = refs[:-2], refs[-2], refs[-1]
    core = lax.axis_index("blk") % 2
    rows = keep.shape[0] - PAD - share
    base = 2 * rows
    bias_rows = split_rows(butterfly_sum([join_rows(a[base + 2 * share :]) for a in arrived]))
    for out, side in ((keep, core), (send, 1 - core)):
        total = sum(a[aligned(side, rows), :].astype(F32) for a in arrived)
        out[:rows] = total.astype(BF16)
        place = pl.ds(pl.multiple_of(base + side * share, PAD), share)
        total = sum(a[place, :].astype(F32) for a in arrived)
        out[rows : rows + share] = total.astype(BF16)
        out[rows + share :] = bias_rows


def core_join_kernel(share, keep, got, *messages):
    zs = len(messages)
    z = lax.axis_index("blk") // 2
    rows = keep.shape[0] - PAD - share
    quarter = rows // zs
    grads = keep[rows : rows + share].astype(F32) + got[rows : rows + share].astype(F32)
    grads = grads.astype(BF16)
    bias_rows = split_rows(join_rows(keep[rows + share :]) + join_rows(got[rows + share :]))
    for k, message in enumerate(messages):
        place = aligned(z ^ k, quarter)
        message[:quarter] = keep[place, :]
        message[quarter : 2 * quarter] = got[place, :]
        message[2 * quarter : 2 * quarter + share] = grads
        message[2 * quarter + share :] = bias_rows


def piece_kernel(*refs):
    arrived, (piece, grad_bias) = refs[:-2], refs[-2:]
    share = piece.shape[0]
    base = arrived[0].shape[0] - PAD - share
    piece[...] = butterfly_sum([a[base : base + share].astype(F32) for a in arrived]).astype(BF16)
    grad_bias[...] = butterfly_sum([join_rows(a[base + share :]) for a in arrived])


def finish_kernel(requests_in, self_term, *refs):
    arrived, (feat_grad, total, requests) = refs[:-3], refs[-3:]
    pltpu.sync_copy(requests_in, requests)
    quarter = total.shape[1]
    blk = lax.axis_index("blk")
    total[...] = self_term[...].reshape(total.shape)
    for k, message in enumerate(arrived):
        for other in range(2):
            block = requests[0, blk ^ (2 * k + other)]
            total[block] += message[other * quarter : (other + 1) * quarter].astype(F32)
    feat_grad[...] = total[...].astype(BF16)


def gather_kernel(*refs):
    pieces, out = refs[:-1], refs[-1]
    share = pieces[0].shape[0]
    rep = lax.axis_index("rep")
    for k, piece in enumerate(pieces):
        out[aligned(rep ^ k, share), :] = piece[...]


def widen_kernel(mine, other, grad_self, grad_neigh):
    core = lax.axis_index("blk") % 2
    first = core == 0
    a = mine[...].astype(F32)
    b = other[...].astype(F32)
    grad_self[...] = jnp.where(first, a, b)
    grad_neigh[...] = jnp.where(first, b, a)


def on_device(feats, requests, tile_dest, tile_slot, tile_vals, w_self, w_neigh, bias, cotangent):
    owners = lax.axis_size("blk")
    replicas = lax.axis_size("rep")
    zs = owners // 2
    blk_dev, width, features = feats.shape
    quarter = width // replicas
    row_count = blk_dev * quarter
    share = features // replicas
    grad_scale = 1.0 / math.sqrt(owners * blk_dev * width)

    outgoing = call(
        pick_kernel,
        [HBM, HBM],
        struct((owners, width, features), BF16),
        VMEM,
        (pltpu.SMEM((1, owners), jnp.int32), pltpu.SemaphoreType.DMA((owners,))),
        name="pick",
        limit=56 * MIB,
    )(requests, feats)
    sources = lax.all_to_all(outgoing, "blk", split_axis=0, concat_axis=0, tiled=True)
    per_slab = row_count // width
    packed = call(
        lambda *refs: prepare_kernel(owners, *refs),
        [SMEM, SMEM, VMEM, HBM, VMEM, VMEM, VMEM],
        struct((2 * (owners // per_slab) + 2, row_count, row_count), BF16),
        VMEM,
        (pltpu.VMEM((blk_dev, quarter, features), BF16), pltpu.SemaphoreType.DMA),
        name="prepare",
    )(tile_dest, tile_slot, tile_vals, feats, w_self, w_neigh, cotangent)

    message_rows = owners * quarter + 2 * share + PAD
    outs = call(
        lambda *refs: layer_kernel(grad_scale, owners, replicas, *refs),
        [VMEM] * 3,
        (struct((row_count, features), F32), struct((row_count, features), BF16))
        + (struct((message_rows, features), BF16),) * replicas,
        (VMEM,) * (2 + replicas),
        (
            pltpu.VMEM((owners, width, features), BF16),
            pltpu.VMEM((2, features, features), BF16),
        ),
        name="layer",
        flops=4 * row_count * features * owners * width,
    )(sources.reshape(owners * width, features), packed, bias.reshape(1, features))
    messages = outs[2:]
    hidden, self_term = call(
        own_kernel,
        [VMEM] * 3,
        (struct((blk_dev, quarter, features), BF16), struct((row_count, features), F32)),
        (VMEM, VMEM),
        name="own",
        flops=2 * row_count * features * features,
    )(outs[0], outs[1], w_self)
    arrived = [messages[0]] + [
        swap(messages[k], "rep", replicas, k) for k in range(1, replicas)
    ]
    arrived[-1], self_term = lax.optimization_barrier((arrived[-1], self_term))
    half = struct((zs * quarter + share + PAD, features), BF16)
    keep, send = call(
        lambda *refs: rep_sum_kernel(share, *refs),
        [VMEM] * replicas,
        (half, half),
        (VMEM, VMEM),
        name="rep_sum",
    )(*arrived)
    got = swap(send, "blk", owners, 1)
    parcels = call(
        lambda *refs: core_join_kernel(share, *refs),
        [VMEM, VMEM],
        (struct((2 * quarter + share + PAD, features), BF16),) * zs,
        (VMEM,) * zs,
        name="core_join",
    )(keep, got)
    landed = [parcels[0]] + [swap(parcels[k], "blk", owners, 2 * k) for k in range(1, zs)]
    piece, grad_bias = call(
        piece_kernel,
        [VMEM] * zs,
        (struct((share, features), BF16), struct((1, features), F32)),
        (VMEM, VMEM),
        name="piece",
    )(*landed)
    feat_grad = call(
        finish_kernel,
        [HBM, VMEM] + [VMEM] * zs,
        struct((blk_dev, quarter, features), BF16),
        VMEM,
        (
            pltpu.VMEM((blk_dev, quarter, features), F32),
            pltpu.SMEM((1, owners), jnp.int32),
        ),
        name="finish",
    )(requests, self_term, *landed)
    pieces = [piece] + [swap(piece, "rep", replicas, k) for k in range(1, replicas)]
    pieces[-1], feat_grad = lax.optimization_barrier((pieces[-1], feat_grad))
    whole = struct((features, features), F32)
    mine = call(
        gather_kernel,
        [VMEM] * replicas,
        struct((features, features), BF16),
        VMEM,
        name="gather_pieces",
    )(*pieces)
    other = swap(mine, "blk", owners, 1)
    grad_self, grad_neigh = call(
        widen_kernel, [VMEM, VMEM], (whole, whole), (VMEM, VMEM), name="widen"
    )(mine, other)
    return (hidden, grad_self, grad_neigh, grad_bias.reshape(features), feat_grad)


def solution(mesh):
    in_specs = (
        P("blk", None, None),
        P("blk", None),
        P("blk", None),
        P("blk", None),
        P("blk", None, "rep", None),
        P(),
        P(),
        P(),
        P("blk", "rep", None),
    )
    out_specs = (P("blk", "rep", None), P(), P(), P(), P("blk", "rep", None))
    return jax.shard_map(
        on_device, mesh=mesh, in_specs=in_specs, out_specs=out_specs, check_vma=False
    )
```

```python
import math

import jax
import jax.numpy as jnp
from jax import lax
from jax.experimental import pallas as pl
from jax.experimental.pallas import tpu as pltpu
from jax.sharding import PartitionSpec as P

BF16 = jnp.bfloat16
F32 = jnp.float32
PAD = 16
MIB = 1024 * 1024
NT = (((1,), (1,)), ((), ()))

VMEM = pl.BlockSpec(memory_space=pltpu.VMEM)
SMEM = pl.BlockSpec(memory_space=pltpu.SMEM)
HBM = pl.BlockSpec(memory_space=pltpu.HBM)


def size_of(array):
    return math.prod(array.shape) * jnp.dtype(array.dtype).itemsize


def call(body, in_specs, out_shape, out_specs, scratch=(), name=None, flops=0, limit=0):
    def run(*operands):
        moved = sum(size_of(a) for a in jax.tree.leaves((operands, out_shape)))
        return pl.pallas_call(
            body,
            in_specs=in_specs,
            out_shape=out_shape,
            out_specs=out_specs,
            scratch_shapes=scratch,
            name=name,
            cost_estimate=pl.CostEstimate(
                flops=flops, bytes_accessed=moved, transcendentals=0
            ),
            compiler_params=pltpu.CompilerParams(
                vmem_limit_bytes=limit or min(moved + moved // 4 + 2 * MIB, 56 * MIB)
            ),
        )(*operands)

    return run


def struct(shape, dtype):
    return jax.ShapeDtypeStruct(shape, dtype)


def aligned(index, size):
    return pl.ds(pl.multiple_of(index * size, size), size)


def dot(a, b):
    return jnp.dot(a, b, preferred_element_type=F32)


def butterfly_sum(terms):
    while len(terms) > 1:
        terms = [terms[i] + terms[i + 1] for i in range(0, len(terms), 2)]
    return terms[0]


def split_rows(row):
    high = row.astype(BF16)
    low = (row - high.astype(F32)).astype(BF16)
    place = lax.broadcasted_iota(jnp.int32, (PAD, row.shape[1]), 0)
    spread = jnp.where(place == 0, high.astype(F32), 0.0)
    spread = jnp.where(place == 1, low.astype(F32), spread)
    return spread.astype(BF16)


def join_rows(rows):
    return jnp.sum(rows.astype(F32), axis=0, keepdims=True)


def swap(array, axis, size, distance):
    return lax.ppermute(array, axis, [(i, i ^ distance) for i in range(size)])


def pick_kernel(requests_in, feats, out, held, requests, sems):
    count = out.shape[0]
    into = pltpu.make_async_copy(feats, held, sems.at[0])
    into.start()
    pltpu.sync_copy(requests_in, requests)
    into.wait()
    away = [
        pltpu.make_async_copy(held.at[requests[0, i]], out.at[i], sems.at[1 + i])
        for i in range(count)
    ]
    for copy in away:
        copy.start()
    for copy in away:
        copy.wait()


def prepare_kernel(
    owners, dest, slot, tiles, feats, w_self, w_neigh, cotangent, packed, rows, sem
):
    tile_count, quarter, width = tiles.shape[1:]
    row_count = packed.shape[1]
    features = w_self.shape[0]
    per_slab = row_count // width
    slabs = owners // per_slab
    rep = lax.axis_index("rep")
    copy = pltpu.make_async_copy(feats.at[:, aligned(rep, quarter), :], rows, sem)
    copy.start()
    packed[:slabs] = jnp.zeros((slabs, row_count, row_count), packed.dtype)

    def place(t, carry):
        owner = slot[0, t]
        packed[
            owner // per_slab, aligned(dest[0, t], quarter), aligned(owner % per_slab, width)
        ] = tiles[0, t]
        return carry

    lax.fori_loop(0, tile_count, place, 0)

    def turn(slab, carry):
        packed[slabs + slab] = packed[slab].T
        return carry

    lax.fori_loop(0, slabs, turn, 0)
    copy.wait()
    own = rows[...].reshape(row_count, features)
    packed[2 * slabs, :, :features] = own
    packed[2 * slabs, :, features:] = cotangent[...].reshape(row_count, features)
    packed[2 * slabs + 1, :features] = own.T
    packed[2 * slabs + 1, features:, :features] = w_self[...]
    packed[2 * slabs + 1, features:, features:] = w_neigh[...]


def layer_kernel(grad_scale, owners, replicas, sources_in, packed, bias, *refs):
    preact_out, grad_pre_out, messages = refs[0], refs[1], refs[2 : 2 + replicas]
    contributions, gradients, sources, sems = refs[2 + replicas :]
    row_count, features = preact_out.shape
    width = contributions.shape[1]
    quarter = width // replicas
    share = features // replicas
    per_slab = row_count // width
    slabs = owners // per_slab
    zs = owners // 2
    rep = lax.axis_index("rep")
    rows = packed[2 * slabs, :, :features]
    cotangent = packed[2 * slabs, :, features:]
    rows_t = packed[2 * slabs + 1, :features]
    w_self = packed[2 * slabs + 1, features:, :features]
    w_neigh = packed[2 * slabs + 1, features:, features:]

    def fetch(slab):
        place = aligned(slab, row_count)
        return pltpu.make_async_copy(sources_in.at[place, :], sources.at[place, :], sems.at[slab])

    for slab in range(slabs):
        fetch(slab).start()
    preact = dot(rows, w_self) + bias[...]
    for slab in range(slabs):
        fetch(slab).wait()
    half = row_count // 2

    def gather_rows(part):
        def add(slab, total):
            return total + dot(packed[slab, part], sources[aligned(slab, row_count), :])

        total = dot(packed[0, part], sources[:row_count])
        return lax.fori_loop(1, slabs, add, total, unroll=slabs <= 4).astype(BF16)

    agg = jnp.concatenate([gather_rows(slice(0, half)), gather_rows(slice(half, row_count))])
    preact += dot(agg, w_neigh)
    preact_out[...] = preact
    gating = jax.nn.sigmoid(preact)
    grad_pre = (
        cotangent.astype(F32) * gating * (1.0 + preact * (1.0 - gating))
    ).astype(BF16)
    grad_pre_out[...] = grad_pre
    back = lax.dot_general(grad_pre, w_neigh, NT, preferred_element_type=F32).astype(BF16)

    def contribute(slab, carry):
        contributions[pl.ds(slab * per_slab, per_slab)] = (
            dot(packed[slabs + slab], back).astype(BF16).reshape(per_slab, width, features)
        )
        return carry

    lax.fori_loop(0, slabs, contribute, 0, unroll=slabs <= 4)
    gradients[0] = (dot(rows_t, grad_pre) * grad_scale).astype(BF16)
    gradients[1] = (dot(agg.T, grad_pre) * grad_scale).astype(BF16)
    bias_rows = split_rows(
        jnp.sum(grad_pre.astype(F32), axis=0, keepdims=True) * grad_scale
    )
    base = owners * quarter
    for k, message in enumerate(messages):
        target = rep ^ k
        for core in range(2):
            for z in range(zs):
                start = (core * zs + z) * quarter
                message[start : start + quarter] = contributions[
                    2 * z + core, aligned(target, quarter), :
                ]
        for half in range(2):
            start = base + half * share
            message[start : start + share] = gradients[half, aligned(target, share), :]
        message[base + 2 * share :] = bias_rows


def own_kernel(preact, grad_pre, w_self, hidden, self_term):
    value = preact[...]
    hidden[...] = (value * jax.nn.sigmoid(value)).astype(BF16).reshape(hidden.shape)
    self_term[...] = lax.dot_general(grad_pre[...], w_self[...], NT, preferred_element_type=F32)


def rep_sum_kernel(share, *refs):
    arrived, keep, send = refs[:-2], refs[-2], refs[-1]
    core = lax.axis_index("blk") % 2
    rows = keep.shape[0] - PAD - share
    base = 2 * rows
    bias_rows = split_rows(butterfly_sum([join_rows(a[base + 2 * share :]) for a in arrived]))
    for out, side in ((keep, core), (send, 1 - core)):
        total = sum(a[aligned(side, rows), :].astype(F32) for a in arrived)
        out[:rows] = total.astype(BF16)
        place = pl.ds(pl.multiple_of(base + side * share, PAD), share)
        total = sum(a[place, :].astype(F32) for a in arrived)
        out[rows : rows + share] = total.astype(BF16)
        out[rows + share :] = bias_rows


def core_join_kernel(share, keep, got, *messages):
    zs = len(messages)
    z = lax.axis_index("blk") // 2
    rows = keep.shape[0] - PAD - share
    quarter = rows // zs
    grads = keep[rows : rows + share].astype(F32) + got[rows : rows + share].astype(F32)
    grads = grads.astype(BF16)
    bias_rows = split_rows(join_rows(keep[rows + share :]) + join_rows(got[rows + share :]))
    for k, message in enumerate(messages):
        place = aligned(z ^ k, quarter)
        message[:quarter] = keep[place, :]
        message[quarter : 2 * quarter] = got[place, :]
        message[2 * quarter : 2 * quarter + share] = grads
        message[2 * quarter + share :] = bias_rows


def piece_kernel(*refs):
    arrived, piece = refs[:-1], refs[-1]
    share = piece.shape[0]
    base = arrived[0].shape[0] - PAD - share
    piece[...] = butterfly_sum([a[base : base + share].astype(F32) for a in arrived]).astype(BF16)


def finish_kernel(requests_in, self_term, *refs):
    arrived, (feat_grad, grad_bias, total, requests) = refs[:-4], refs[-4:]
    pltpu.sync_copy(requests_in, requests)
    grad_bias[...] = butterfly_sum([join_rows(a[a.shape[0] - PAD :]) for a in arrived])
    quarter = total.shape[1]
    blk = lax.axis_index("blk")
    total[...] = self_term[...].reshape(total.shape)
    for k, message in enumerate(arrived):
        for other in range(2):
            block = requests[0, blk ^ (2 * k + other)]
            total[block] += message[other * quarter : (other + 1) * quarter].astype(F32)
    feat_grad[...] = total[...].astype(BF16)


def gather_kernel(*refs):
    pieces, out = refs[:-1], refs[-1]
    share = pieces[0].shape[0]
    rep = lax.axis_index("rep")
    for k, piece in enumerate(pieces):
        out[aligned(rep ^ k, share), :] = piece[...]


def widen_kernel(mine, other, grad_self, grad_neigh):
    core = lax.axis_index("blk") % 2
    first = core == 0
    a = mine[...].astype(F32)
    b = other[...].astype(F32)
    grad_self[...] = jnp.where(first, a, b)
    grad_neigh[...] = jnp.where(first, b, a)


def on_device(feats, requests, tile_dest, tile_slot, tile_vals, w_self, w_neigh, bias, cotangent):
    owners = lax.axis_size("blk")
    replicas = lax.axis_size("rep")
    zs = owners // 2
    blk_dev, width, features = feats.shape
    quarter = width // replicas
    row_count = blk_dev * quarter
    share = features // replicas
    grad_scale = 1.0 / math.sqrt(owners * blk_dev * width)

    outgoing = call(
        pick_kernel,
        [HBM, HBM],
        struct((owners, width, features), BF16),
        HBM,
        (
            pltpu.VMEM(feats.shape, BF16),
            pltpu.SMEM((1, owners), jnp.int32),
            pltpu.SemaphoreType.DMA((1 + owners,)),
        ),
        name="pick",
        limit=56 * MIB,
    )(requests, feats)
    sources = lax.all_to_all(outgoing, "blk", split_axis=0, concat_axis=0, tiled=True)
    per_slab = row_count // width
    packed = call(
        lambda *refs: prepare_kernel(owners, *refs),
        [SMEM, SMEM, VMEM, HBM, VMEM, VMEM, VMEM],
        struct((2 * (owners // per_slab) + 2, row_count, row_count), BF16),
        VMEM,
        (pltpu.VMEM((blk_dev, quarter, features), BF16), pltpu.SemaphoreType.DMA),
        name="prepare",
    )(tile_dest, tile_slot, tile_vals, feats, w_self, w_neigh, cotangent)

    message_rows = owners * quarter + 2 * share + PAD
    outs = call(
        lambda *refs: layer_kernel(grad_scale, owners, replicas, *refs),
        [HBM, VMEM, VMEM],
        (struct((row_count, features), F32), struct((row_count, features), BF16))
        + (struct((message_rows, features), BF16),) * replicas,
        (VMEM,) * (2 + replicas),
        (
            pltpu.VMEM((owners, width, features), BF16),
            pltpu.VMEM((2, features, features), BF16),
            pltpu.VMEM((owners * width, features), BF16),
            pltpu.SemaphoreType.DMA((owners // per_slab,)),
        ),
        name="layer",
        flops=4 * row_count * features * owners * width,
    )(sources.reshape(owners * width, features), packed, bias.reshape(1, features))
    messages = outs[2:]
    hidden, self_term = call(
        own_kernel,
        [VMEM] * 3,
        (struct((blk_dev, quarter, features), BF16), struct((row_count, features), F32)),
        (VMEM, VMEM),
        name="own",
        flops=2 * row_count * features * features,
    )(outs[0], outs[1], w_self)
    arrived = [messages[0]] + [
        swap(messages[k], "rep", replicas, k) for k in range(1, replicas)
    ]
    arrived[-1], self_term = lax.optimization_barrier((arrived[-1], self_term))
    half = struct((zs * quarter + share + PAD, features), BF16)
    keep, send = call(
        lambda *refs: rep_sum_kernel(share, *refs),
        [VMEM] * replicas,
        (half, half),
        (VMEM, VMEM),
        name="rep_sum",
    )(*arrived)
    got = swap(send, "blk", owners, 1)
    parcels = call(
        lambda *refs: core_join_kernel(share, *refs),
        [VMEM, VMEM],
        (struct((2 * quarter + share + PAD, features), BF16),) * zs,
        (VMEM,) * zs,
        name="core_join",
    )(keep, got)
    landed = [parcels[0]] + [swap(parcels[k], "blk", owners, 2 * k) for k in range(1, zs)]
    landed[-1], hidden = lax.optimization_barrier((landed[-1], hidden))
    piece = call(
        piece_kernel, [VMEM] * zs, struct((share, features), BF16), VMEM, name="piece"
    )(*landed)
    feat_grad, grad_bias = call(
        finish_kernel,
        [HBM, VMEM] + [VMEM] * zs,
        (struct((blk_dev, quarter, features), BF16), struct((1, features), F32)),
        (VMEM, VMEM),
        (
            pltpu.VMEM((blk_dev, quarter, features), F32),
            pltpu.SMEM((1, owners), jnp.int32),
        ),
        name="finish",
    )(requests, self_term, *landed)
    pieces = [piece] + [swap(piece, "rep", replicas, k) for k in range(1, replicas)]
    whole = struct((features, features), F32)
    mine = call(
        gather_kernel,
        [VMEM] * replicas,
        struct((features, features), BF16),
        VMEM,
        name="gather_pieces",
    )(*pieces)
    other = swap(mine, "blk", owners, 1)
    other, feat_grad = lax.optimization_barrier((other, feat_grad))
    grad_self, grad_neigh = call(
        widen_kernel, [VMEM, VMEM], (whole, whole), (VMEM, VMEM), name="widen"
    )(mine, other)
    return (hidden, grad_self, grad_neigh, grad_bias.reshape(features), feat_grad)


def solution(mesh):
    in_specs = (
        P("blk", None, None),
        P("blk", None),
        P("blk", None),
        P("blk", None),
        P("blk", None, "rep", None),
        P(),
        P(),
        P(),
        P("blk", "rep", None),
    )
    out_specs = (P("blk", "rep", None), P(), P(), P(), P("blk", "rep", None))
    return jax.shard_map(
        on_device, mesh=mesh, in_specs=in_specs, out_specs=out_specs, check_vma=False
    )
```

```python
import math

import jax
import jax.numpy as jnp
from jax import lax
from jax.experimental import pallas as pl
from jax.experimental.pallas import tpu as pltpu
from jax.sharding import PartitionSpec as P

BF16 = jnp.bfloat16
F32 = jnp.float32
PAD = 16
MIB = 1024 * 1024
NT = (((1,), (1,)), ((), ()))

VMEM = pl.BlockSpec(memory_space=pltpu.VMEM)
SMEM = pl.BlockSpec(memory_space=pltpu.SMEM)
HBM = pl.BlockSpec(memory_space=pltpu.HBM)


def size_of(array):
    return math.prod(array.shape) * jnp.dtype(array.dtype).itemsize


def call(body, in_specs, out_shape, out_specs, scratch=(), name=None, flops=0, limit=0):
    def run(*operands):
        moved = sum(size_of(a) for a in jax.tree.leaves((operands, out_shape)))
        return pl.pallas_call(
            body,
            in_specs=in_specs,
            out_shape=out_shape,
            out_specs=out_specs,
            scratch_shapes=scratch,
            name=name,
            cost_estimate=pl.CostEstimate(
                flops=flops, bytes_accessed=moved, transcendentals=0
            ),
            compiler_params=pltpu.CompilerParams(
                vmem_limit_bytes=limit or min(moved + moved // 4 + 2 * MIB, 56 * MIB)
            ),
        )(*operands)

    return run


def struct(shape, dtype):
    return jax.ShapeDtypeStruct(shape, dtype)


def aligned(index, size):
    return pl.ds(pl.multiple_of(index * size, size), size)


def dot(a, b):
    return jnp.dot(a, b, preferred_element_type=F32)


def butterfly_sum(terms):
    while len(terms) > 1:
        terms = [terms[i] + terms[i + 1] for i in range(0, len(terms), 2)]
    return terms[0]


def split_rows(row):
    high = row.astype(BF16)
    low = (row - high.astype(F32)).astype(BF16)
    place = lax.broadcasted_iota(jnp.int32, (PAD, row.shape[1]), 0)
    spread = jnp.where(place == 0, high.astype(F32), 0.0)
    spread = jnp.where(place == 1, low.astype(F32), spread)
    return spread.astype(BF16)


def join_rows(rows):
    return jnp.sum(rows.astype(F32), axis=0, keepdims=True)


def swap(array, axis, size, distance):
    return lax.ppermute(array, axis, [(i, i ^ distance) for i in range(size)])


def pick_kernel(requests_in, feats, keep, send, held, requests, sem):
    copy = pltpu.make_async_copy(feats, held, sem)
    copy.start()
    pltpu.sync_copy(requests_in, requests)
    copy.wait()
    blk = lax.axis_index("blk")
    for k in range(keep.shape[0]):
        keep[k] = held[requests[0, blk ^ (2 * k)]]
        send[k] = held[requests[0, blk ^ (2 * k + 1)]]


def join_kernel(keep, got, *messages):
    for k, message in enumerate(messages):
        message[0] = keep[k]
        message[1] = got[k]


def prepare_kernel(
    owners, dest, slot, tiles, feats, w_self, w_neigh, cotangent, packed, rows, sem
):
    tile_count, quarter, width = tiles.shape[1:]
    row_count = packed.shape[1]
    features = w_self.shape[0]
    per_slab = row_count // width
    slabs = owners // per_slab
    rep, blk = lax.axis_index("rep"), lax.axis_index("blk")
    copy = pltpu.make_async_copy(feats.at[:, aligned(rep, quarter), :], rows, sem)
    copy.start()
    packed[:slabs] = jnp.zeros((slabs, row_count, row_count), packed.dtype)

    def place(t, carry):
        owner = slot[0, t] ^ blk
        packed[
            owner // per_slab, aligned(dest[0, t], quarter), aligned(owner % per_slab, width)
        ] = tiles[0, t]
        return carry

    lax.fori_loop(0, tile_count, place, 0)

    def turn(slab, carry):
        packed[slabs + slab] = packed[slab].T
        return carry

    lax.fori_loop(0, slabs, turn, 0)
    copy.wait()
    own = rows[...].reshape(row_count, features)
    packed[2 * slabs, :, :features] = own
    packed[2 * slabs, :, features:] = cotangent[...].reshape(row_count, features)
    packed[2 * slabs + 1, :features] = own.T
    packed[2 * slabs + 1, features:, :features] = w_self[...]
    packed[2 * slabs + 1, features:, features:] = w_neigh[...]


def layer_kernel(grad_scale, packed, bias, *refs):
    arrived, (preact_out, grad_pre_out, keep, send) = refs[:-4], refs[-4:]
    row_count, features = preact_out.shape
    zs = len(arrived)
    width = arrived[0].shape[1]
    pair = 2 * width
    per_slab = row_count // pair
    slabs = zs // per_slab
    rows = packed[2 * slabs, :, :features]
    cotangent = packed[2 * slabs, :, features:]
    rows_t = packed[2 * slabs + 1, :features]
    w_self = packed[2 * slabs + 1, features:, :features]
    w_neigh = packed[2 * slabs + 1, features:, features:]
    half = row_count // 2

    def gather_rows(part):
        total = jnp.zeros((half, features), F32)
        for k, message in enumerate(arrived):
            lanes = slice(k % per_slab * pair, (k % per_slab + 1) * pair)
            total += dot(packed[k // per_slab, part, lanes], message[...].reshape(pair, features))
        return total.astype(BF16)

    agg = jnp.concatenate([gather_rows(slice(0, half)), gather_rows(slice(half, row_count))])
    preact = dot(rows, w_self) + bias[...] + dot(agg, w_neigh)
    preact_out[...] = preact
    gating = jax.nn.sigmoid(preact)
    grad_pre = (
        cotangent.astype(F32) * gating * (1.0 + preact * (1.0 - gating))
    ).astype(BF16)
    grad_pre_out[...] = grad_pre
    back = lax.dot_general(grad_pre, w_neigh, NT, preferred_element_type=F32).astype(BF16)

    def contribute(slab, carry):
        block = dot(packed[slabs + slab], back).astype(BF16)
        for i in range(per_slab):
            place = aligned(slab * per_slab + i, width)
            keep[place, :] = block[i * pair : i * pair + width]
            send[place, :] = block[i * pair + width : (i + 1) * pair]
        return carry

    lax.fori_loop(0, slabs, contribute, 0, unroll=slabs <= 4)
    base = zs * width
    grad_self = (dot(rows_t, grad_pre) * grad_scale).astype(BF16)
    grad_neigh = (dot(agg.T, grad_pre) * grad_scale).astype(BF16)
    bias_rows = split_rows(
        jnp.sum(grad_pre.astype(F32), axis=0, keepdims=True) * grad_scale
    )
    core = lax.axis_index("blk") % 2
    for side, to_self, to_neigh in ((0, keep, send), (1, send, keep)):

        @pl.when(core == side)
        def _():
            to_self[base : base + features] = grad_self
            to_neigh[base : base + features] = grad_neigh

    keep[base + features :] = bias_rows
    send[base + features :] = bias_rows


def own_kernel(preact, grad_pre, w_self, hidden, self_term):
    value = preact[...]
    hidden[...] = (value * jax.nn.sigmoid(value)).astype(BF16).reshape(hidden.shape)
    self_term[...] = lax.dot_general(grad_pre[...], w_self[...], NT, preferred_element_type=F32)


def assemble_kernel(zs, keep, got, *refs):
    messages, gradients = refs[:-1], refs[-1]
    replicas = len(messages)
    features = keep.shape[1]
    base = keep.shape[0] - PAD - features
    width = base // zs
    quarter, share = width // replicas, features // replicas
    end = 2 * zs * quarter
    rep = lax.axis_index("rep")
    grads = slice(base, base + features)
    gradients[...] = (keep[grads].astype(F32) + got[grads].astype(F32)).astype(BF16)
    bias_rows = split_rows(join_rows(keep[base + features :]) + join_rows(got[base + features :]))
    for k, message in enumerate(messages):
        target = rep ^ k
        for z in range(zs):
            place = pl.ds(pl.multiple_of(z * width + target * quarter, quarter), quarter)
            start = 2 * z * quarter
            message[start : start + quarter] = keep[place, :]
            message[start + quarter : start + 2 * quarter] = got[place, :]
        message[end : end + share] = gradients[aligned(target, share), :]
        message[end + share :] = bias_rows


def rep_sum_kernel(zs, *refs):
    arrived, parcels = refs[:-zs], refs[-zs:]
    rows = (arrived[0].shape[0] - parcels[0].shape[0]) // (zs - 1)
    share = parcels[0].shape[0] - PAD - rows
    end = zs * rows
    grads = sum(a[end : end + share].astype(F32) for a in arrived).astype(BF16)
    bias_rows = split_rows(butterfly_sum([join_rows(a[end + share :]) for a in arrived]))
    for k, parcel in enumerate(parcels):
        place = slice(k * rows, (k + 1) * rows)
        parcel[:rows] = sum(a[place].astype(F32) for a in arrived).astype(BF16)
        parcel[rows : rows + share] = grads
        parcel[rows + share :] = bias_rows


def piece_kernel(*refs):
    arrived, piece = refs[:-1], refs[-1]
    share = piece.shape[0]
    base = arrived[0].shape[0] - PAD - share
    piece[...] = butterfly_sum([a[base : base + share].astype(F32) for a in arrived]).astype(BF16)


def finish_kernel(requests_in, self_term, *refs):
    arrived, (feat_grad, grad_bias, total, requests) = refs[:-4], refs[-4:]
    pltpu.sync_copy(requests_in, requests)
    grad_bias[...] = butterfly_sum([join_rows(a[a.shape[0] - PAD :]) for a in arrived])
    quarter = total.shape[1]
    blk = lax.axis_index("blk")
    total[...] = self_term[...].reshape(total.shape)
    for k, message in enumerate(arrived):
        for other in range(2):
            block = requests[0, blk ^ (2 * k + other)]
            total[block] += message[other * quarter : (other + 1) * quarter].astype(F32)
    feat_grad[...] = total[...].astype(BF16)


def gather_kernel(*refs):
    pieces, out = refs[:-1], refs[-1]
    share = pieces[0].shape[0]
    rep = lax.axis_index("rep")
    for k, piece in enumerate(pieces):
        out[aligned(rep ^ k, share), :] = piece[...]


def widen_kernel(mine, other, grad_self, grad_neigh):
    core = lax.axis_index("blk") % 2
    first = core == 0
    a = mine[...].astype(F32)
    b = other[...].astype(F32)
    grad_self[...] = jnp.where(first, a, b)
    grad_neigh[...] = jnp.where(first, b, a)


def on_device(feats, requests, tile_dest, tile_slot, tile_vals, w_self, w_neigh, bias, cotangent):
    owners = lax.axis_size("blk")
    replicas = lax.axis_size("rep")
    zs = owners // 2
    blk_dev, width, features = feats.shape
    quarter = width // replicas
    row_count = blk_dev * quarter
    share = features // replicas
    grad_scale = 1.0 / math.sqrt(owners * blk_dev * width)

    blocks = struct((zs, width, features), BF16)
    keep, send = call(
        pick_kernel,
        [HBM, HBM],
        (blocks, blocks),
        (VMEM, VMEM),
        (
            pltpu.VMEM(feats.shape, BF16),
            pltpu.SMEM((1, owners), jnp.int32),
            pltpu.SemaphoreType.DMA,
        ),
        name="pick",
        limit=53 * MIB,
    )(requests, feats)
    got = swap(send, "blk", owners, 1)
    messages = call(
        join_kernel,
        [VMEM, VMEM],
        (struct((2, width, features), BF16),) * zs,
        (VMEM,) * zs,
        name="join",
    )(keep, got)
    sources = [messages[0]] + [swap(messages[k], "blk", owners, 2 * k) for k in range(1, zs)]
    per_slab = row_count // width
    packed = call(
        lambda *refs: prepare_kernel(owners, *refs),
        [SMEM, SMEM, VMEM, HBM, VMEM, VMEM, VMEM],
        struct((2 * (owners // per_slab) + 2, row_count, row_count), BF16),
        VMEM,
        (pltpu.VMEM((blk_dev, quarter, features), BF16), pltpu.SemaphoreType.DMA),
        name="prepare",
    )(tile_dest, tile_slot, tile_vals, feats, w_self, w_neigh, cotangent)

    half = struct((zs * width + features + PAD, features), BF16)
    preact, grad_pre, keep, send = call(
        lambda *refs: layer_kernel(grad_scale, *refs),
        [VMEM] * (2 + zs),
        (struct((row_count, features), F32), struct((row_count, features), BF16), half, half),
        (VMEM,) * 4,
        name="layer",
        flops=4 * row_count * features * owners * width,
    )(packed, bias.reshape(1, features), *sources)
    got = swap(send, "blk", owners, 1)
    messages = call(
        lambda *refs: assemble_kernel(zs, *refs),
        [VMEM, VMEM],
        (struct((2 * zs * quarter + share + PAD, features), BF16),) * replicas,
        (VMEM,) * replicas,
        (pltpu.VMEM((features, features), BF16),),
        name="assemble",
    )(keep, got)
    hidden, self_term = call(
        own_kernel,
        [VMEM] * 3,
        (struct((blk_dev, quarter, features), BF16), struct((row_count, features), F32)),
        (VMEM, VMEM),
        name="own",
        flops=2 * row_count * features * features,
    )(preact, grad_pre, w_self)
    arrived = [messages[0]] + [
        swap(messages[k], "rep", replicas, k) for k in range(1, replicas)
    ]
    arrived[-1], self_term = lax.optimization_barrier((arrived[-1], self_term))
    parcels = call(
        lambda *refs: rep_sum_kernel(zs, *refs),
        [VMEM] * replicas,
        (struct((2 * quarter + share + PAD, features), BF16),) * zs,
        (VMEM,) * zs,
        name="rep_sum",
    )(*arrived)
    landed = [parcels[0]] + [swap(parcels[k], "blk", owners, 2 * k) for k in range(1, zs)]
    landed[-1], hidden = lax.optimization_barrier((landed[-1], hidden))
    piece = call(
        piece_kernel, [VMEM] * zs, struct((share, features), BF16), VMEM, name="piece"
    )(*landed)
    feat_grad, grad_bias = call(
        finish_kernel,
        [HBM, VMEM] + [VMEM] * zs,
        (struct((blk_dev, quarter, features), BF16), struct((1, features), F32)),
        (VMEM, VMEM),
        (
            pltpu.VMEM((blk_dev, quarter, features), F32),
            pltpu.SMEM((1, owners), jnp.int32),
        ),
        name="finish",
    )(requests, self_term, *landed)
    pieces = [piece] + [swap(piece, "rep", replicas, k) for k in range(1, replicas)]
    whole = struct((features, features), F32)
    mine = call(
        gather_kernel,
        [VMEM] * replicas,
        struct((features, features), BF16),
        VMEM,
        name="gather_pieces",
    )(*pieces)
    other = swap(mine, "blk", owners, 1)
    other, feat_grad = lax.optimization_barrier((other, feat_grad))
    grad_self, grad_neigh = call(
        widen_kernel, [VMEM, VMEM], (whole, whole), (VMEM, VMEM), name="widen"
    )(mine, other)
    return (hidden, grad_self, grad_neigh, grad_bias.reshape(features), feat_grad)


def solution(mesh):
    in_specs = (
        P("blk", None, None),
        P("blk", None),
        P("blk", None),
        P("blk", None),
        P("blk", None, "rep", None),
        P(),
        P(),
        P(),
        P("blk", "rep", None),
    )
    out_specs = (P("blk", "rep", None), P(), P(), P(), P("blk", "rep", None))
    return jax.shard_map(
        on_device, mesh=mesh, in_specs=in_specs, out_specs=out_specs, check_vma=False
    )
```

```python
import math

import jax
import jax.numpy as jnp
from jax import lax
from jax.experimental import pallas as pl
from jax.experimental.pallas import tpu as pltpu
from jax.sharding import PartitionSpec as P

BF16 = jnp.bfloat16
F32 = jnp.float32
PAD = 16
MIB = 1024 * 1024
NT = (((1,), (1,)), ((), ()))

VMEM = pl.BlockSpec(memory_space=pltpu.VMEM)
SMEM = pl.BlockSpec(memory_space=pltpu.SMEM)
HBM = pl.BlockSpec(memory_space=pltpu.HBM)


def size_of(array):
    return math.prod(array.shape) * jnp.dtype(array.dtype).itemsize


def call(body, in_specs, out_shape, out_specs, scratch=(), name=None, flops=0, limit=0):
    def run(*operands):
        moved = sum(size_of(a) for a in jax.tree.leaves((operands, out_shape)))
        return pl.pallas_call(
            body,
            in_specs=in_specs,
            out_shape=out_shape,
            out_specs=out_specs,
            scratch_shapes=scratch,
            name=name,
            cost_estimate=pl.CostEstimate(
                flops=flops, bytes_accessed=moved, transcendentals=0
            ),
            compiler_params=pltpu.CompilerParams(
                vmem_limit_bytes=limit or min(moved + moved // 4 + 2 * MIB, 56 * MIB)
            ),
        )(*operands)

    return run


def struct(shape, dtype):
    return jax.ShapeDtypeStruct(shape, dtype)


def aligned(index, size):
    return pl.ds(pl.multiple_of(index * size, size), size)


def dot(a, b):
    return jnp.dot(a, b, preferred_element_type=F32)


def butterfly_sum(terms):
    while len(terms) > 1:
        terms = [terms[i] + terms[i + 1] for i in range(0, len(terms), 2)]
    return terms[0]


def split_rows(row):
    high = row.astype(BF16)
    low = (row - high.astype(F32)).astype(BF16)
    place = lax.broadcasted_iota(jnp.int32, (PAD, row.shape[1]), 0)
    spread = jnp.where(place == 0, high.astype(F32), 0.0)
    spread = jnp.where(place == 1, low.astype(F32), spread)
    return spread.astype(BF16)


def join_rows(rows):
    return jnp.sum(rows.astype(F32), axis=0, keepdims=True)


def swap(array, axis, size, distance):
    return lax.ppermute(array, axis, [(i, i ^ distance) for i in range(size)])


def pick_kernel(requests_in, feats, keep, send, held, requests, sem):
    copy = pltpu.make_async_copy(feats, held, sem)
    copy.start()
    pltpu.sync_copy(requests_in, requests)
    copy.wait()
    blk = lax.axis_index("blk")
    for k in range(keep.shape[0]):
        keep[k] = held[requests[0, blk ^ (2 * k)]]
        send[k] = held[requests[0, blk ^ (2 * k + 1)]]


def join_kernel(keep, got, *messages):
    for k, message in enumerate(messages):
        message[0] = keep[k]
        message[1] = got[k]


def prepare_kernel(
    owners, dest, slot, tiles, feats, w_self, w_neigh, cotangent, packed, rows, sem
):
    tile_count, quarter, width = tiles.shape[1:]
    row_count = packed.shape[1]
    features = w_self.shape[0]
    per_slab = row_count // width
    slabs = owners // per_slab
    rep, blk = lax.axis_index("rep"), lax.axis_index("blk")
    copy = pltpu.make_async_copy(feats.at[:, aligned(rep, quarter), :], rows, sem)
    copy.start()
    packed[:slabs] = jnp.zeros((slabs, row_count, row_count), packed.dtype)

    def place(t, carry):
        owner = slot[0, t] ^ blk
        packed[
            owner // per_slab, aligned(dest[0, t], quarter), aligned(owner % per_slab, width)
        ] = tiles[0, t]
        return carry

    lax.fori_loop(0, tile_count, place, 0)

    def turn(slab, carry):
        packed[slabs + slab] = packed[slab].T
        return carry

    lax.fori_loop(0, slabs, turn, 0)
    copy.wait()
    own = rows[...].reshape(row_count, features)
    packed[2 * slabs, :, :features] = own
    packed[2 * slabs, :, features:] = cotangent[...].reshape(row_count, features)
    packed[2 * slabs + 1, :features] = own.T
    packed[2 * slabs + 1, features:, :features] = w_self[...]
    packed[2 * slabs + 1, features:, features:] = w_neigh[...]


def layer_kernel(grad_scale, packed, bias, *refs):
    arrived, (preact_out, grad_pre_out, keep, send) = refs[:-4], refs[-4:]
    row_count, features = preact_out.shape
    zs = len(arrived)
    width = arrived[0].shape[1]
    pair = 2 * width
    per_slab = row_count // pair
    slabs = zs // per_slab
    rows = packed[2 * slabs, :, :features]
    cotangent = packed[2 * slabs, :, features:]
    rows_t = packed[2 * slabs + 1, :features]
    w_self = packed[2 * slabs + 1, features:, :features]
    w_neigh = packed[2 * slabs + 1, features:, features:]
    half = row_count // 2

    def gather_rows(part):
        total = jnp.zeros((half, features), F32)
        for k, message in enumerate(arrived):
            lanes = slice(k % per_slab * pair, (k % per_slab + 1) * pair)
            total += dot(packed[k // per_slab, part, lanes], message[...].reshape(pair, features))
        return total.astype(BF16)

    agg = jnp.concatenate([gather_rows(slice(0, half)), gather_rows(slice(half, row_count))])
    preact = dot(rows, w_self) + bias[...] + dot(agg, w_neigh)
    preact_out[...] = preact
    gating = jax.nn.sigmoid(preact)
    grad_pre = (
        cotangent.astype(F32) * gating * (1.0 + preact * (1.0 - gating))
    ).astype(BF16)
    grad_pre_out[...] = grad_pre
    back = lax.dot_general(grad_pre, w_neigh, NT, preferred_element_type=F32).astype(BF16)

    def contribute(slab, carry):
        block = dot(packed[slabs + slab], back).astype(BF16)
        for i in range(per_slab):
            place = aligned(slab * per_slab + i, width)
            keep[place, :] = block[i * pair : i * pair + width]
            send[place, :] = block[i * pair + width : (i + 1) * pair]
        return carry

    lax.fori_loop(0, slabs, contribute, 0, unroll=slabs <= 4)
    base = zs * width
    grad_self = (dot(rows_t, grad_pre) * grad_scale).astype(BF16)
    grad_neigh = (dot(agg.T, grad_pre) * grad_scale).astype(BF16)
    bias_rows = split_rows(
        jnp.sum(grad_pre.astype(F32), axis=0, keepdims=True) * grad_scale
    )
    core = lax.axis_index("blk") % 2
    for side, to_self, to_neigh in ((0, keep, send), (1, send, keep)):

        @pl.when(core == side)
        def _():
            to_self[base : base + features] = grad_self
            to_neigh[base : base + features] = grad_neigh

    keep[base + features :] = bias_rows
    send[base + features :] = bias_rows


def own_kernel(preact, grad_pre, w_self, hidden, self_term):
    value = preact[...]
    hidden[...] = (value * jax.nn.sigmoid(value)).astype(BF16).reshape(hidden.shape)
    self_term[...] = lax.dot_general(grad_pre[...], w_self[...], NT, preferred_element_type=F32)


def assemble_kernel(zs, keep, got, *refs):
    messages, gradients = refs[:-1], refs[-1]
    replicas = len(messages)
    features = keep.shape[1]
    base = keep.shape[0] - PAD - features
    width = base // zs
    quarter, share = width // replicas, features // replicas
    end = 2 * zs * quarter
    rep = lax.axis_index("rep")
    grads = slice(base, base + features)
    gradients[...] = (keep[grads].astype(F32) + got[grads].astype(F32)).astype(BF16)
    bias_rows = split_rows(join_rows(keep[base + features :]) + join_rows(got[base + features :]))
    for k, message in enumerate(messages):
        target = rep ^ k
        for z in range(zs):
            place = pl.ds(pl.multiple_of(z * width + target * quarter, quarter), quarter)
            start = 2 * z * quarter
            message[start : start + quarter] = keep[place, :]
            message[start + quarter : start + 2 * quarter] = got[place, :]
        message[end : end + share] = gradients[aligned(target, share), :]
        message[end + share :] = bias_rows


def rep_sum_kernel(zs, *refs):
    arrived, parcels = refs[:-zs], refs[-zs:]
    rows = (arrived[0].shape[0] - parcels[0].shape[0]) // (zs - 1)
    share = parcels[0].shape[0] - PAD - rows
    end = zs * rows
    grads = sum(a[end : end + share].astype(F32) for a in arrived).astype(BF16)
    bias_rows = split_rows(butterfly_sum([join_rows(a[end + share :]) for a in arrived]))
    for k, parcel in enumerate(parcels):
        place = slice(k * rows, (k + 1) * rows)
        parcel[:rows] = sum(a[place].astype(F32) for a in arrived).astype(BF16)
        parcel[rows : rows + share] = grads
        parcel[rows + share :] = bias_rows


def piece_kernel(*refs):
    arrived, piece = refs[:-1], refs[-1]
    share = piece.shape[0]
    base = arrived[0].shape[0] - PAD - share
    piece[...] = butterfly_sum([a[base : base + share].astype(F32) for a in arrived]).astype(BF16)


def finish_kernel(requests_in, self_term, *refs):
    arrived, (feat_grad, grad_bias, total, requests) = refs[:-4], refs[-4:]
    pltpu.sync_copy(requests_in, requests)
    grad_bias[...] = butterfly_sum([join_rows(a[a.shape[0] - PAD :]) for a in arrived])
    quarter = total.shape[1]
    blk = lax.axis_index("blk")
    total[...] = self_term[...].reshape(total.shape)
    for k, message in enumerate(arrived):
        for other in range(2):
            block = requests[0, blk ^ (2 * k + other)]
            total[block] += message[other * quarter : (other + 1) * quarter].astype(F32)
    feat_grad[...] = total[...].astype(BF16)


def gather_kernel(*refs):
    pieces, out = refs[:-1], refs[-1]
    share = pieces[0].shape[0]
    rep = lax.axis_index("rep")
    for k, piece in enumerate(pieces):
        out[aligned(rep ^ k, share), :] = piece[...]


def widen_kernel(mine, other, grad_self, grad_neigh):
    core = lax.axis_index("blk") % 2
    first = core == 0
    a = mine[...].astype(F32)
    b = other[...].astype(F32)
    grad_self[...] = jnp.where(first, a, b)
    grad_neigh[...] = jnp.where(first, b, a)


def on_device(feats, requests, tile_dest, tile_slot, tile_vals, w_self, w_neigh, bias, cotangent):
    owners = lax.axis_size("blk")
    replicas = lax.axis_size("rep")
    zs = owners // 2
    blk_dev, width, features = feats.shape
    quarter = width // replicas
    row_count = blk_dev * quarter
    share = features // replicas
    grad_scale = 1.0 / math.sqrt(owners * blk_dev * width)

    blocks = struct((zs, width, features), BF16)
    keep, send = call(
        pick_kernel,
        [HBM, HBM],
        (blocks, blocks),
        (VMEM, VMEM),
        (
            pltpu.VMEM(feats.shape, BF16),
            pltpu.SMEM((1, owners), jnp.int32),
            pltpu.SemaphoreType.DMA,
        ),
        name="pick",
        limit=53 * MIB,
    )(requests, feats)
    got = swap(send, "blk", owners, 1)
    messages = call(
        join_kernel,
        [VMEM, VMEM],
        (struct((2, width, features), BF16),) * zs,
        (VMEM,) * zs,
        name="join",
    )(keep, got)
    sources = [messages[0]] + [swap(messages[k], "blk", owners, 2 * k) for k in range(1, zs)]
    per_slab = row_count // width
    packed = call(
        lambda *refs: prepare_kernel(owners, *refs),
        [SMEM, SMEM, VMEM, HBM, VMEM, VMEM, VMEM],
        struct((2 * (owners // per_slab) + 2, row_count, row_count), BF16),
        VMEM,
        (pltpu.VMEM((blk_dev, quarter, features), BF16), pltpu.SemaphoreType.DMA),
        name="prepare",
    )(tile_dest, tile_slot, tile_vals, feats, w_self, w_neigh, cotangent)

    sources[-1], packed = lax.optimization_barrier((sources[-1], packed))
    half = struct((zs * width + features + PAD, features), BF16)
    preact, grad_pre, keep, send = call(
        lambda *refs: layer_kernel(grad_scale, *refs),
        [VMEM] * (2 + zs),
        (struct((row_count, features), F32), struct((row_count, features), BF16), half, half),
        (VMEM,) * 4,
        name="layer",
        flops=4 * row_count * features * owners * width,
    )(packed, bias.reshape(1, features), *sources)
    got = swap(send, "blk", owners, 1)
    messages = call(
        lambda *refs: assemble_kernel(zs, *refs),
        [VMEM, VMEM],
        (struct((2 * zs * quarter + share + PAD, features), BF16),) * replicas,
        (VMEM,) * replicas,
        (pltpu.VMEM((features, features), BF16),),
        name="assemble",
    )(keep, got)
    hidden, self_term = call(
        own_kernel,
        [VMEM] * 3,
        (struct((blk_dev, quarter, features), BF16), struct((row_count, features), F32)),
        (VMEM, VMEM),
        name="own",
        flops=2 * row_count * features * features,
    )(preact, grad_pre, w_self)
    arrived = [messages[0]] + [
        swap(messages[k], "rep", replicas, k) for k in range(1, replicas)
    ]
    *arrived, self_term = lax.optimization_barrier((*arrived, self_term))
    parcels = call(
        lambda *refs: rep_sum_kernel(zs, *refs),
        [VMEM] * replicas,
        (struct((2 * quarter + share + PAD, features), BF16),) * zs,
        (VMEM,) * zs,
        name="rep_sum",
    )(*arrived)
    landed = [parcels[0]] + [swap(parcels[k], "blk", owners, 2 * k) for k in range(1, zs)]
    landed[-1], hidden = lax.optimization_barrier((landed[-1], hidden))
    piece = call(
        piece_kernel, [VMEM] * zs, struct((share, features), BF16), VMEM, name="piece"
    )(*landed)
    feat_grad, grad_bias = call(
        finish_kernel,
        [HBM, VMEM] + [VMEM] * zs,
        (struct((blk_dev, quarter, features), BF16), struct((1, features), F32)),
        (VMEM, VMEM),
        (
            pltpu.VMEM((blk_dev, quarter, features), F32),
            pltpu.SMEM((1, owners), jnp.int32),
        ),
        name="finish",
    )(requests, self_term, *landed)
    pieces = [piece] + [swap(piece, "rep", replicas, k) for k in range(1, replicas)]
    whole = struct((features, features), F32)
    mine = call(
        gather_kernel,
        [VMEM] * replicas,
        struct((features, features), BF16),
        VMEM,
        name="gather_pieces",
    )(*pieces)
    other = swap(mine, "blk", owners, 1)
    other, feat_grad = lax.optimization_barrier((other, feat_grad))
    grad_self, grad_neigh = call(
        widen_kernel, [VMEM, VMEM], (whole, whole), (VMEM, VMEM), name="widen"
    )(mine, other)
    return (hidden, grad_self, grad_neigh, grad_bias.reshape(features), feat_grad)


def solution(mesh):
    in_specs = (
        P("blk", None, None),
        P("blk", None),
        P("blk", None),
        P("blk", None),
        P("blk", None, "rep", None),
        P(),
        P(),
        P(),
        P("blk", "rep", None),
    )
    out_specs = (P("blk", "rep", None), P(), P(), P(), P("blk", "rep", None))
    return jax.shard_map(
        on_device, mesh=mesh, in_specs=in_specs, out_specs=out_specs, check_vma=False
    )
```

```python
import math

import jax
import jax.numpy as jnp
from jax import lax
from jax.experimental import pallas as pl
from jax.experimental.pallas import tpu as pltpu
from jax.sharding import PartitionSpec as P

BF16 = jnp.bfloat16
F32 = jnp.float32
PAD = 16
MIB = 1024 * 1024
NT = (((1,), (1,)), ((), ()))

VMEM = pl.BlockSpec(memory_space=pltpu.VMEM)
SMEM = pl.BlockSpec(memory_space=pltpu.SMEM)
HBM = pl.BlockSpec(memory_space=pltpu.HBM)


def size_of(array):
    return math.prod(array.shape) * jnp.dtype(array.dtype).itemsize


def call(body, in_specs, out_shape, out_specs, scratch=(), name=None, flops=0, limit=0):
    def run(*operands):
        moved = sum(size_of(a) for a in jax.tree.leaves((operands, out_shape)))
        return pl.pallas_call(
            body,
            in_specs=in_specs,
            out_shape=out_shape,
            out_specs=out_specs,
            scratch_shapes=scratch,
            name=name,
            cost_estimate=pl.CostEstimate(
                flops=flops, bytes_accessed=moved, transcendentals=0
            ),
            compiler_params=pltpu.CompilerParams(
                vmem_limit_bytes=limit or min(moved + moved // 4 + 2 * MIB, 56 * MIB)
            ),
        )(*operands)

    return run


def struct(shape, dtype):
    return jax.ShapeDtypeStruct(shape, dtype)


def aligned(index, size):
    return pl.ds(pl.multiple_of(index * size, size), size)


def dot(a, b):
    return jnp.dot(a, b, preferred_element_type=F32)


def butterfly_sum(terms):
    while len(terms) > 1:
        terms = [terms[i] + terms[i + 1] for i in range(0, len(terms), 2)]
    return terms[0]


def split_rows(row):
    high = row.astype(BF16)
    low = (row - high.astype(F32)).astype(BF16)
    place = lax.broadcasted_iota(jnp.int32, (PAD, row.shape[1]), 0)
    spread = jnp.where(place == 0, high.astype(F32), 0.0)
    spread = jnp.where(place == 1, low.astype(F32), spread)
    return spread.astype(BF16)


def join_rows(rows):
    return jnp.sum(rows.astype(F32), axis=0, keepdims=True)


def split_halves(row):
    lanes = row.shape[1] // 2
    high = row.astype(BF16).astype(F32)
    low = row - high
    place = lax.broadcasted_iota(jnp.int32, (PAD, lanes), 0)
    spread = jnp.zeros((PAD, lanes), F32)
    for i, part in enumerate((high[:, :lanes], high[:, lanes:], low[:, :lanes], low[:, lanes:])):
        spread = jnp.where(place == i, part, spread)
    return spread.astype(BF16)


def join_halves(rows):
    rows = rows.astype(F32)
    place = lax.broadcasted_iota(jnp.int32, rows.shape, 0)
    left = jnp.sum(jnp.where(place % 2 == 0, rows, 0.0), axis=0, keepdims=True)
    right = jnp.sum(jnp.where(place % 2 == 1, rows, 0.0), axis=0, keepdims=True)
    return jnp.concatenate([left, right], axis=1)


def put(message, start, block):
    rows = (message.shape[0] - PAD) // 2
    count, lanes = block.shape[0], message.shape[1]
    message[start : start + count] = block[:, :lanes]
    message[rows + start : rows + start + count] = block[:, lanes:]


def swap(array, axis, size, distance):
    return lax.ppermute(array, axis, [(i, i ^ distance) for i in range(size)])


def pick_kernel(requests_in, feats, keep, send, held, requests, sem):
    copy = pltpu.make_async_copy(feats, held, sem)
    copy.start()
    pltpu.sync_copy(requests_in, requests)
    copy.wait()
    blk = lax.axis_index("blk")
    for k in range(keep.shape[0]):
        keep[k] = held[requests[0, blk ^ (2 * k)]]
        send[k] = held[requests[0, blk ^ (2 * k + 1)]]


def join_kernel(keep, got, *messages):
    for k, message in enumerate(messages):
        message[0] = keep[k]
        message[1] = got[k]


def prepare_kernel(
    owners, dest, slot, tiles, feats, w_self, w_neigh, cotangent, packed, rows, sem
):
    tile_count, quarter, width = tiles.shape[1:]
    row_count = packed.shape[1]
    features = w_self.shape[0]
    per_slab = row_count // width
    slabs = owners // per_slab
    rep, blk = lax.axis_index("rep"), lax.axis_index("blk")
    copy = pltpu.make_async_copy(feats.at[:, aligned(rep, quarter), :], rows, sem)
    copy.start()
    packed[:slabs] = jnp.zeros((slabs, row_count, row_count), packed.dtype)

    def place(t, carry):
        owner = slot[0, t] ^ blk
        packed[
            owner // per_slab, aligned(dest[0, t], quarter), aligned(owner % per_slab, width)
        ] = tiles[0, t]
        return carry

    lax.fori_loop(0, tile_count, place, 0)

    def turn(slab, carry):
        packed[slabs + slab] = packed[slab].T
        return carry

    lax.fori_loop(0, slabs, turn, 0)
    copy.wait()
    own = rows[...].reshape(row_count, features)
    packed[2 * slabs, :, :features] = own
    packed[2 * slabs, :, features:] = cotangent[...].reshape(row_count, features)
    packed[2 * slabs + 1, :features] = own.T
    packed[2 * slabs + 1, features:, :features] = w_self[...]
    packed[2 * slabs + 1, features:, features:] = w_neigh[...]


def layer_kernel(grad_scale, packed, bias, *refs):
    arrived, (preact_out, grad_pre_out, keep, send) = refs[:-4], refs[-4:]
    row_count, features = preact_out.shape
    zs = len(arrived)
    width = arrived[0].shape[1]
    pair = 2 * width
    per_slab = row_count // pair
    slabs = zs // per_slab
    rows = packed[2 * slabs, :, :features]
    cotangent = packed[2 * slabs, :, features:]
    rows_t = packed[2 * slabs + 1, :features]
    w_self = packed[2 * slabs + 1, features:, :features]
    w_neigh = packed[2 * slabs + 1, features:, features:]
    half = row_count // 2

    def gather_rows(part):
        total = jnp.zeros((half, features), F32)
        for k, message in enumerate(arrived):
            lanes = slice(k % per_slab * pair, (k % per_slab + 1) * pair)
            total += dot(packed[k // per_slab, part, lanes], message[...].reshape(pair, features))
        return total.astype(BF16)

    agg = jnp.concatenate([gather_rows(slice(0, half)), gather_rows(slice(half, row_count))])
    preact = dot(rows, w_self) + bias[...] + dot(agg, w_neigh)
    preact_out[...] = preact
    gating = jax.nn.sigmoid(preact)
    grad_pre = (
        cotangent.astype(F32) * gating * (1.0 + preact * (1.0 - gating))
    ).astype(BF16)
    grad_pre_out[...] = grad_pre
    back = lax.dot_general(grad_pre, w_neigh, NT, preferred_element_type=F32).astype(BF16)

    def contribute(slab, carry):
        block = dot(packed[slabs + slab], back).astype(BF16)
        for i in range(per_slab):
            place = aligned(slab * per_slab + i, width)
            keep[place, :] = block[i * pair : i * pair + width]
            send[place, :] = block[i * pair + width : (i + 1) * pair]
        return carry

    lax.fori_loop(0, slabs, contribute, 0, unroll=slabs <= 4)
    base = zs * width
    grad_self = (dot(rows_t, grad_pre) * grad_scale).astype(BF16)
    grad_neigh = (dot(agg.T, grad_pre) * grad_scale).astype(BF16)
    bias_rows = split_rows(
        jnp.sum(grad_pre.astype(F32), axis=0, keepdims=True) * grad_scale
    )
    core = lax.axis_index("blk") % 2
    for side, to_self, to_neigh in ((0, keep, send), (1, send, keep)):

        @pl.when(core == side)
        def _():
            to_self[base : base + features] = grad_self
            to_neigh[base : base + features] = grad_neigh

    keep[base + features :] = bias_rows
    send[base + features :] = bias_rows


def own_kernel(preact, grad_pre, w_self, hidden, self_term):
    value = preact[...]
    hidden[...] = (value * jax.nn.sigmoid(value)).astype(BF16).reshape(hidden.shape)
    self_term[...] = lax.dot_general(grad_pre[...], w_self[...], NT, preferred_element_type=F32)


def assemble_kernel(zs, keep, got, *refs):
    messages, gradients = refs[:-1], refs[-1]
    replicas = len(messages)
    features = keep.shape[1]
    base = keep.shape[0] - PAD - features
    width = base // zs
    quarter, share = width // replicas, features // replicas
    end = 2 * zs * quarter
    rep = lax.axis_index("rep")
    grads = slice(base, base + features)
    gradients[...] = (keep[grads].astype(F32) + got[grads].astype(F32)).astype(BF16)
    bias_rows = split_halves(
        join_rows(keep[base + features :]) + join_rows(got[base + features :])
    )
    for k, message in enumerate(messages):
        target = rep ^ k
        for z in range(zs):
            place = pl.ds(pl.multiple_of(z * width + target * quarter, quarter), quarter)
            start = 2 * z * quarter
            put(message, start, keep[place, :])
            put(message, start + quarter, got[place, :])
        put(message, end, gradients[aligned(target, share), :])
        message[2 * (end + share) :] = bias_rows


def rep_sum_kernel(zs, *refs):
    arrived, parcels = refs[:-zs], refs[-zs:]
    taken, given = (arrived[0].shape[0] - PAD) // 2, (parcels[0].shape[0] - PAD) // 2
    rows = (taken - given) // (zs - 1)
    bias_rows = split_halves(butterfly_sum([join_halves(a[2 * taken :]) for a in arrived]))
    for side in range(2):
        grads = slice(side * taken + zs * rows, (side + 1) * taken)
        grads = sum(a[grads].astype(F32) for a in arrived).astype(BF16)
        for k, parcel in enumerate(parcels):
            place = slice(side * taken + k * rows, side * taken + (k + 1) * rows)
            start = side * given
            parcel[start : start + rows] = sum(a[place].astype(F32) for a in arrived).astype(BF16)
            parcel[start + rows : start + given] = grads
    for parcel in parcels:
        parcel[2 * given :] = bias_rows


def piece_kernel(*refs):
    arrived, piece = refs[:-1], refs[-1]
    share, lanes = piece.shape[0], arrived[0].shape[1]
    given = (arrived[0].shape[0] - PAD) // 2
    for side in range(2):
        place = slice((side + 1) * given - share, (side + 1) * given)
        total = butterfly_sum([a[place].astype(F32) for a in arrived])
        piece[:, side * lanes : (side + 1) * lanes] = total.astype(BF16)


def finish_kernel(requests_in, self_term, *refs):
    arrived, (feat_grad, grad_bias, total, requests) = refs[:-4], refs[-4:]
    pltpu.sync_copy(requests_in, requests)
    grad_bias[...] = butterfly_sum([join_halves(a[a.shape[0] - PAD :]) for a in arrived])
    quarter, lanes = total.shape[1], arrived[0].shape[1]
    given = (arrived[0].shape[0] - PAD) // 2
    blk = lax.axis_index("blk")
    total[...] = self_term[...].reshape(total.shape)
    for k, message in enumerate(arrived):
        for other in range(2):
            block = requests[0, blk ^ (2 * k + other)]
            for side in range(2):
                start = side * given + other * quarter
                part = message[start : start + quarter].astype(F32)
                total[block, :, side * lanes : (side + 1) * lanes] += part
    feat_grad[...] = total[...].astype(BF16)


def gather_kernel(*refs):
    pieces, out = refs[:-1], refs[-1]
    share = pieces[0].shape[0]
    rep = lax.axis_index("rep")
    for k, piece in enumerate(pieces):
        out[aligned(rep ^ k, share), :] = piece[...]


def widen_kernel(mine, other, grad_self, grad_neigh):
    core = lax.axis_index("blk") % 2
    first = core == 0
    a = mine[...].astype(F32)
    b = other[...].astype(F32)
    grad_self[...] = jnp.where(first, a, b)
    grad_neigh[...] = jnp.where(first, b, a)


def on_device(feats, requests, tile_dest, tile_slot, tile_vals, w_self, w_neigh, bias, cotangent):
    owners = lax.axis_size("blk")
    replicas = lax.axis_size("rep")
    zs = owners // 2
    blk_dev, width, features = feats.shape
    quarter = width // replicas
    row_count = blk_dev * quarter
    share = features // replicas
    grad_scale = 1.0 / math.sqrt(owners * blk_dev * width)

    blocks = struct((zs, width, features), BF16)
    keep, send = call(
        pick_kernel,
        [HBM, HBM],
        (blocks, blocks),
        (VMEM, VMEM),
        (
            pltpu.VMEM(feats.shape, BF16),
            pltpu.SMEM((1, owners), jnp.int32),
            pltpu.SemaphoreType.DMA,
        ),
        name="pick",
        limit=53 * MIB,
    )(requests, feats)
    got = swap(send, "blk", owners, 1)
    messages = call(
        join_kernel,
        [VMEM, VMEM],
        (struct((2, width, features), BF16),) * zs,
        (VMEM,) * zs,
        name="join",
    )(keep, got)
    sources = [messages[0]] + [swap(messages[k], "blk", owners, 2 * k) for k in range(1, zs)]
    per_slab = row_count // width
    packed = call(
        lambda *refs: prepare_kernel(owners, *refs),
        [SMEM, SMEM, VMEM, HBM, VMEM, VMEM, VMEM],
        struct((2 * (owners // per_slab) + 2, row_count, row_count), BF16),
        VMEM,
        (pltpu.VMEM((blk_dev, quarter, features), BF16), pltpu.SemaphoreType.DMA),
        name="prepare",
    )(tile_dest, tile_slot, tile_vals, feats, w_self, w_neigh, cotangent)

    sources[-1], packed = lax.optimization_barrier((sources[-1], packed))
    half = struct((zs * width + features + PAD, features), BF16)
    preact, grad_pre, keep, send = call(
        lambda *refs: layer_kernel(grad_scale, *refs),
        [VMEM] * (2 + zs),
        (struct((row_count, features), F32), struct((row_count, features), BF16), half, half),
        (VMEM,) * 4,
        name="layer",
        flops=4 * row_count * features * owners * width,
    )(packed, bias.reshape(1, features), *sources)
    got = swap(send, "blk", owners, 1)
    messages = call(
        lambda *refs: assemble_kernel(zs, *refs),
        [VMEM, VMEM],
        (struct((2 * (2 * zs * quarter + share) + PAD, features // 2), BF16),) * replicas,
        (VMEM,) * replicas,
        (pltpu.VMEM((features, features), BF16),),
        name="assemble",
    )(keep, got)
    hidden, self_term = call(
        own_kernel,
        [VMEM] * 3,
        (struct((blk_dev, quarter, features), BF16), struct((row_count, features), F32)),
        (VMEM, VMEM),
        name="own",
        flops=2 * row_count * features * features,
    )(preact, grad_pre, w_self)
    arrived = [messages[0]] + [
        swap(messages[k], "rep", replicas, k) for k in range(1, replicas)
    ]
    *arrived, self_term = lax.optimization_barrier((*arrived, self_term))
    parcels = call(
        lambda *refs: rep_sum_kernel(zs, *refs),
        [VMEM] * replicas,
        (struct((2 * (2 * quarter + share) + PAD, features // 2), BF16),) * zs,
        (VMEM,) * zs,
        name="rep_sum",
    )(*arrived)
    landed = [parcels[0]] + [swap(parcels[k], "blk", owners, 2 * k) for k in range(1, zs)]
    landed[-1], hidden = lax.optimization_barrier((landed[-1], hidden))
    piece = call(
        piece_kernel, [VMEM] * zs, struct((share, features), BF16), VMEM, name="piece"
    )(*landed)
    feat_grad, grad_bias = call(
        finish_kernel,
        [HBM, VMEM] + [VMEM] * zs,
        (struct((blk_dev, quarter, features), BF16), struct((1, features), F32)),
        (VMEM, VMEM),
        (
            pltpu.VMEM((blk_dev, quarter, features), F32),
            pltpu.SMEM((1, owners), jnp.int32),
        ),
        name="finish",
    )(requests, self_term, *landed)
    pieces = [piece] + [swap(piece, "rep", replicas, k) for k in range(1, replicas)]
    whole = struct((features, features), F32)
    mine = call(
        gather_kernel,
        [VMEM] * replicas,
        struct((features, features), BF16),
        VMEM,
        name="gather_pieces",
    )(*pieces)
    other = swap(mine, "blk", owners, 1)
    other, feat_grad = lax.optimization_barrier((other, feat_grad))
    grad_self, grad_neigh = call(
        widen_kernel, [VMEM, VMEM], (whole, whole), (VMEM, VMEM), name="widen"
    )(mine, other)
    return (hidden, grad_self, grad_neigh, grad_bias.reshape(features), feat_grad)


def solution(mesh):
    in_specs = (
        P("blk", None, None),
        P("blk", None),
        P("blk", None),
        P("blk", None),
        P("blk", None, "rep", None),
        P(),
        P(),
        P(),
        P("blk", "rep", None),
    )
    out_specs = (P("blk", "rep", None), P(), P(), P(), P("blk", "rep", None))
    return jax.shard_map(
        on_device, mesh=mesh, in_specs=in_specs, out_specs=out_specs, check_vma=False
    )
```

```python
import math

import jax
import jax.numpy as jnp
from jax import lax
from jax.experimental import pallas as pl
from jax.experimental.pallas import tpu as pltpu
from jax.sharding import PartitionSpec as P

BF16 = jnp.bfloat16
F32 = jnp.float32
PAD = 16
MIB = 1024 * 1024
NT = (((1,), (1,)), ((), ()))

VMEM = pl.BlockSpec(memory_space=pltpu.VMEM)
SMEM = pl.BlockSpec(memory_space=pltpu.SMEM)
HBM = pl.BlockSpec(memory_space=pltpu.HBM)


def size_of(array):
    return math.prod(array.shape) * jnp.dtype(array.dtype).itemsize


def call(body, in_specs, out_shape, out_specs, scratch=(), name=None, flops=0, limit=0):
    def run(*operands):
        moved = sum(size_of(a) for a in jax.tree.leaves((operands, out_shape)))
        return pl.pallas_call(
            body,
            in_specs=in_specs,
            out_shape=out_shape,
            out_specs=out_specs,
            scratch_shapes=scratch,
            name=name,
            cost_estimate=pl.CostEstimate(
                flops=flops, bytes_accessed=moved, transcendentals=0
            ),
            compiler_params=pltpu.CompilerParams(
                vmem_limit_bytes=limit or min(moved + moved // 4 + 2 * MIB, 56 * MIB)
            ),
        )(*operands)

    return run


def struct(shape, dtype):
    return jax.ShapeDtypeStruct(shape, dtype)


def aligned(index, size):
    return pl.ds(pl.multiple_of(index * size, size), size)


def dot(a, b):
    return jnp.dot(a, b, preferred_element_type=F32)


def butterfly_sum(terms):
    while len(terms) > 1:
        terms = [terms[i] + terms[i + 1] for i in range(0, len(terms), 2)]
    return terms[0]


def split_rows(row):
    high = row.astype(BF16)
    low = (row - high.astype(F32)).astype(BF16)
    place = lax.broadcasted_iota(jnp.int32, (PAD, row.shape[1]), 0)
    spread = jnp.where(place == 0, high.astype(F32), 0.0)
    spread = jnp.where(place == 1, low.astype(F32), spread)
    return spread.astype(BF16)


def join_rows(rows):
    return jnp.sum(rows.astype(F32), axis=0, keepdims=True)


def split_halves(row):
    lanes = row.shape[1] // 2
    high = row.astype(BF16).astype(F32)
    low = row - high
    place = lax.broadcasted_iota(jnp.int32, (PAD, lanes), 0)
    spread = jnp.zeros((PAD, lanes), F32)
    for i, part in enumerate((high[:, :lanes], high[:, lanes:], low[:, :lanes], low[:, lanes:])):
        spread = jnp.where(place == i, part, spread)
    return spread.astype(BF16)


def join_halves(rows):
    rows = rows.astype(F32)
    place = lax.broadcasted_iota(jnp.int32, rows.shape, 0)
    left = jnp.sum(jnp.where(place % 2 == 0, rows, 0.0), axis=0, keepdims=True)
    right = jnp.sum(jnp.where(place % 2 == 1, rows, 0.0), axis=0, keepdims=True)
    return jnp.concatenate([left, right], axis=1)


def put(message, start, block):
    rows = (message.shape[0] - PAD) // 2
    count, lanes = block.shape[0], message.shape[1]
    message[start : start + count] = block[:, :lanes]
    message[rows + start : rows + start + count] = block[:, lanes:]


def flipped(k, zs):
    return k // (zs // 2)


def swap(array, axis, size, distance):
    return lax.ppermute(array, axis, [(i, i ^ distance) for i in range(size)])


def pick_kernel(requests_in, feats, keep, send, held, requests, sem):
    copy = pltpu.make_async_copy(feats, held, sem)
    copy.start()
    pltpu.sync_copy(requests_in, requests)
    copy.wait()
    blk = lax.axis_index("blk")
    for k in range(keep.shape[0]):
        flip = flipped(k, keep.shape[0])
        keep[k] = held[requests[0, blk ^ (2 * k + flip)]]
        send[k] = held[requests[0, blk ^ (2 * k + 1 - flip)]]


def join_kernel(keep, got, *messages):
    for k, message in enumerate(messages):
        flip = flipped(k, len(messages))
        message[flip] = keep[k]
        message[1 - flip] = got[k]


def prepare_kernel(
    owners, dest, slot, tiles, feats, w_self, w_neigh, cotangent, packed, rows, sem
):
    tile_count, quarter, width = tiles.shape[1:]
    row_count = packed.shape[1]
    features = w_self.shape[0]
    per_slab = row_count // width
    slabs = owners // per_slab
    rep, blk = lax.axis_index("rep"), lax.axis_index("blk")
    copy = pltpu.make_async_copy(feats.at[:, aligned(rep, quarter), :], rows, sem)
    copy.start()
    packed[:slabs] = jnp.zeros((slabs, row_count, row_count), packed.dtype)

    def place(t, carry):
        owner = slot[0, t] ^ blk
        packed[
            owner // per_slab, aligned(dest[0, t], quarter), aligned(owner % per_slab, width)
        ] = tiles[0, t]
        return carry

    lax.fori_loop(0, tile_count, place, 0)

    def turn(slab, carry):
        packed[slabs + slab] = packed[slab].T
        return carry

    lax.fori_loop(0, slabs, turn, 0)
    copy.wait()
    own = rows[...].reshape(row_count, features)
    packed[2 * slabs, :, :features] = own
    packed[2 * slabs, :, features:] = cotangent[...].reshape(row_count, features)
    packed[2 * slabs + 1, :features] = own.T
    packed[2 * slabs + 1, features:, :features] = w_self[...]
    packed[2 * slabs + 1, features:, features:] = w_neigh[...]


def layer_kernel(grad_scale, packed, bias, *refs):
    arrived, (preact_out, grad_pre_out, keep, send) = refs[:-4], refs[-4:]
    row_count, features = preact_out.shape
    zs = len(arrived)
    width = arrived[0].shape[1]
    pair = 2 * width
    per_slab = row_count // pair
    slabs = zs // per_slab
    rows = packed[2 * slabs, :, :features]
    cotangent = packed[2 * slabs, :, features:]
    rows_t = packed[2 * slabs + 1, :features]
    w_self = packed[2 * slabs + 1, features:, :features]
    w_neigh = packed[2 * slabs + 1, features:, features:]
    half = row_count // 2

    def gather_rows(part):
        total = jnp.zeros((half, features), F32)
        for k, message in enumerate(arrived):
            lanes = slice(k % per_slab * pair, (k % per_slab + 1) * pair)
            total += dot(packed[k // per_slab, part, lanes], message[...].reshape(pair, features))
        return total.astype(BF16)

    agg = jnp.concatenate([gather_rows(slice(0, half)), gather_rows(slice(half, row_count))])
    preact = dot(rows, w_self) + bias[...] + dot(agg, w_neigh)
    preact_out[...] = preact
    gating = jax.nn.sigmoid(preact)
    grad_pre = (
        cotangent.astype(F32) * gating * (1.0 + preact * (1.0 - gating))
    ).astype(BF16)
    grad_pre_out[...] = grad_pre
    back = lax.dot_general(grad_pre, w_neigh, NT, preferred_element_type=F32).astype(BF16)

    def contribute(slab, carry):
        block = dot(packed[slabs + slab], back).astype(BF16)
        for i in range(per_slab):
            place = aligned(slab * per_slab + i, width)
            keep[place, :] = block[i * pair : i * pair + width]
            send[place, :] = block[i * pair + width : (i + 1) * pair]
        return carry

    lax.fori_loop(0, slabs, contribute, 0, unroll=slabs <= 4)
    base = zs * width
    grad_self = (dot(rows_t, grad_pre) * grad_scale).astype(BF16)
    grad_neigh = (dot(agg.T, grad_pre) * grad_scale).astype(BF16)
    bias_rows = split_rows(
        jnp.sum(grad_pre.astype(F32), axis=0, keepdims=True) * grad_scale
    )
    core = lax.axis_index("blk") % 2
    for side, to_self, to_neigh in ((0, keep, send), (1, send, keep)):

        @pl.when(core == side)
        def _():
            to_self[base : base + features] = grad_self
            to_neigh[base : base + features] = grad_neigh

    keep[base + features :] = bias_rows
    send[base + features :] = bias_rows


def own_kernel(preact, grad_pre, w_self, hidden, self_term):
    value = preact[...]
    hidden[...] = (value * jax.nn.sigmoid(value)).astype(BF16).reshape(hidden.shape)
    self_term[...] = lax.dot_general(grad_pre[...], w_self[...], NT, preferred_element_type=F32)


def assemble_kernel(zs, keep, got, *refs):
    messages, gradients = refs[:-1], refs[-1]
    replicas = len(messages)
    features = keep.shape[1]
    base = keep.shape[0] - PAD - features
    width = base // zs
    quarter, share = width // replicas, features // replicas
    end = 2 * zs * quarter
    rep = lax.axis_index("rep")
    grads = slice(base, base + features)
    gradients[...] = (keep[grads].astype(F32) + got[grads].astype(F32)).astype(BF16)
    bias_rows = split_halves(
        join_rows(keep[base + features :]) + join_rows(got[base + features :])
    )
    for k, message in enumerate(messages):
        target = rep ^ k
        for z in range(zs):
            place = pl.ds(pl.multiple_of(z * width + target * quarter, quarter), quarter)
            start = 2 * z * quarter
            put(message, start, keep[place, :])
            put(message, start + quarter, got[place, :])
        put(message, end, gradients[aligned(target, share), :])
        message[2 * (end + share) :] = bias_rows


def rep_sum_kernel(zs, *refs):
    arrived, parcels = refs[:-zs], refs[-zs:]
    taken, given = (arrived[0].shape[0] - PAD) // 2, (parcels[0].shape[0] - PAD) // 2
    rows = (taken - given) // (zs - 1)
    bias_rows = split_halves(butterfly_sum([join_halves(a[2 * taken :]) for a in arrived]))
    for side in range(2):
        grads = slice(side * taken + zs * rows, (side + 1) * taken)
        grads = sum(a[grads].astype(F32) for a in arrived).astype(BF16)
        for k, parcel in enumerate(parcels):
            place = slice(side * taken + k * rows, side * taken + (k + 1) * rows)
            start = side * given
            parcel[start : start + rows] = sum(a[place].astype(F32) for a in arrived).astype(BF16)
            parcel[start + rows : start + given] = grads
    for parcel in parcels:
        parcel[2 * given :] = bias_rows


def piece_kernel(*refs):
    arrived, piece = refs[:-1], refs[-1]
    share, lanes = piece.shape[0], arrived[0].shape[1]
    given = (arrived[0].shape[0] - PAD) // 2
    for side in range(2):
        place = slice((side + 1) * given - share, (side + 1) * given)
        total = butterfly_sum([a[place].astype(F32) for a in arrived])
        piece[:, side * lanes : (side + 1) * lanes] = total.astype(BF16)


def finish_kernel(requests_in, self_term, *refs):
    arrived, (feat_grad, grad_bias, total, requests) = refs[:-4], refs[-4:]
    pltpu.sync_copy(requests_in, requests)
    grad_bias[...] = butterfly_sum([join_halves(a[a.shape[0] - PAD :]) for a in arrived])
    quarter, lanes = total.shape[1], arrived[0].shape[1]
    given = (arrived[0].shape[0] - PAD) // 2
    blk = lax.axis_index("blk")
    total[...] = self_term[...].reshape(total.shape)
    for k, message in enumerate(arrived):
        for other in range(2):
            block = requests[0, blk ^ (2 * k + other)]
            for side in range(2):
                start = side * given + other * quarter
                part = message[start : start + quarter].astype(F32)
                total[block, :, side * lanes : (side + 1) * lanes] += part
    feat_grad[...] = total[...].astype(BF16)


def gather_kernel(*refs):
    pieces, out = refs[:-1], refs[-1]
    share = pieces[0].shape[0]
    rep = lax.axis_index("rep")
    for k, piece in enumerate(pieces):
        out[aligned(rep ^ k, share), :] = piece[...]


def widen_kernel(mine, other, grad_self, grad_neigh):
    core = lax.axis_index("blk") % 2
    first = core == 0
    a = mine[...].astype(F32)
    b = other[...].astype(F32)
    grad_self[...] = jnp.where(first, a, b)
    grad_neigh[...] = jnp.where(first, b, a)


def on_device(feats, requests, tile_dest, tile_slot, tile_vals, w_self, w_neigh, bias, cotangent):
    owners = lax.axis_size("blk")
    replicas = lax.axis_size("rep")
    zs = owners // 2
    blk_dev, width, features = feats.shape
    quarter = width // replicas
    row_count = blk_dev * quarter
    share = features // replicas
    grad_scale = 1.0 / math.sqrt(owners * blk_dev * width)

    blocks = struct((zs, width, features), BF16)
    keep, send = call(
        pick_kernel,
        [HBM, HBM],
        (blocks, blocks),
        (VMEM, VMEM),
        (
            pltpu.VMEM(feats.shape, BF16),
            pltpu.SMEM((1, owners), jnp.int32),
            pltpu.SemaphoreType.DMA,
        ),
        name="pick",
        limit=53 * MIB,
    )(requests, feats)
    got = swap(send, "blk", owners, 1)
    messages = call(
        join_kernel,
        [VMEM, VMEM],
        (struct((2, width, features), BF16),) * zs,
        (VMEM,) * zs,
        name="join",
    )(keep, got)
    sources = [messages[0]] + [
        swap(messages[k], "blk", owners, 2 * k + flipped(k, zs)) for k in range(1, zs)
    ]
    per_slab = row_count // width
    packed = call(
        lambda *refs: prepare_kernel(owners, *refs),
        [SMEM, SMEM, VMEM, HBM, VMEM, VMEM, VMEM],
        struct((2 * (owners // per_slab) + 2, row_count, row_count), BF16),
        VMEM,
        (pltpu.VMEM((blk_dev, quarter, features), BF16), pltpu.SemaphoreType.DMA),
        name="prepare",
    )(tile_dest, tile_slot, tile_vals, feats, w_self, w_neigh, cotangent)

    sources[-1], packed = lax.optimization_barrier((sources[-1], packed))
    half = struct((zs * width + features + PAD, features), BF16)
    preact, grad_pre, keep, send = call(
        lambda *refs: layer_kernel(grad_scale, *refs),
        [VMEM] * (2 + zs),
        (struct((row_count, features), F32), struct((row_count, features), BF16), half, half),
        (VMEM,) * 4,
        name="layer",
        flops=4 * row_count * features * owners * width,
    )(packed, bias.reshape(1, features), *sources)
    got = swap(send, "blk", owners, 1)
    messages = call(
        lambda *refs: assemble_kernel(zs, *refs),
        [VMEM, VMEM],
        (struct((2 * (2 * zs * quarter + share) + PAD, features // 2), BF16),) * replicas,
        (VMEM,) * replicas,
        (pltpu.VMEM((features, features), BF16),),
        name="assemble",
    )(keep, got)
    hidden, self_term = call(
        own_kernel,
        [VMEM] * 3,
        (struct((blk_dev, quarter, features), BF16), struct((row_count, features), F32)),
        (VMEM, VMEM),
        name="own",
        flops=2 * row_count * features * features,
    )(preact, grad_pre, w_self)
    arrived = [messages[0]] + [
        swap(messages[k], "rep", replicas, k) for k in range(1, replicas)
    ]
    *arrived, self_term = lax.optimization_barrier((*arrived, self_term))
    parcels = call(
        lambda *refs: rep_sum_kernel(zs, *refs),
        [VMEM] * replicas,
        (struct((2 * (2 * quarter + share) + PAD, features // 2), BF16),) * zs,
        (VMEM,) * zs,
        name="rep_sum",
    )(*arrived)
    landed = [parcels[0]] + [swap(parcels[k], "blk", owners, 2 * k) for k in range(1, zs)]
    landed[-1], hidden = lax.optimization_barrier((landed[-1], hidden))
    piece = call(
        piece_kernel, [VMEM] * zs, struct((share, features), BF16), VMEM, name="piece"
    )(*landed)
    feat_grad, grad_bias = call(
        finish_kernel,
        [HBM, VMEM] + [VMEM] * zs,
        (struct((blk_dev, quarter, features), BF16), struct((1, features), F32)),
        (VMEM, VMEM),
        (
            pltpu.VMEM((blk_dev, quarter, features), F32),
            pltpu.SMEM((1, owners), jnp.int32),
        ),
        name="finish",
    )(requests, self_term, *landed)
    pieces = [piece] + [swap(piece, "rep", replicas, k) for k in range(1, replicas)]
    *pieces, feat_grad = lax.optimization_barrier((*pieces, feat_grad))
    whole = struct((features, features), F32)
    mine = call(
        gather_kernel,
        [VMEM] * replicas,
        struct((features, features), BF16),
        VMEM,
        name="gather_pieces",
    )(*pieces)
    other = swap(mine, "blk", owners, 1)
    other, feat_grad = lax.optimization_barrier((other, feat_grad))
    grad_self, grad_neigh = call(
        widen_kernel, [VMEM, VMEM], (whole, whole), (VMEM, VMEM), name="widen"
    )(mine, other)
    return (hidden, grad_self, grad_neigh, grad_bias.reshape(features), feat_grad)


def solution(mesh):
    in_specs = (
        P("blk", None, None),
        P("blk", None),
        P("blk", None),
        P("blk", None),
        P("blk", None, "rep", None),
        P(),
        P(),
        P(),
        P("blk", "rep", None),
    )
    out_specs = (P("blk", "rep", None), P(), P(), P(), P("blk", "rep", None))
    return jax.shard_map(
        on_device, mesh=mesh, in_specs=in_specs, out_specs=out_specs, check_vma=False
    )
```

```python
import math

import jax
import jax.numpy as jnp
from jax import lax
from jax.experimental import pallas as pl
from jax.experimental.pallas import tpu as pltpu
from jax.sharding import PartitionSpec as P

BF16 = jnp.bfloat16
F32 = jnp.float32
PAD = 16
MIB = 1024 * 1024
NT = (((1,), (1,)), ((), ()))

VMEM = pl.BlockSpec(memory_space=pltpu.VMEM)
SMEM = pl.BlockSpec(memory_space=pltpu.SMEM)
HBM = pl.BlockSpec(memory_space=pltpu.HBM)


def size_of(array):
    return math.prod(array.shape) * jnp.dtype(array.dtype).itemsize


def call(body, in_specs, out_shape, out_specs, scratch=(), name=None, flops=0, limit=0):
    def run(*operands):
        moved = sum(size_of(a) for a in jax.tree.leaves((operands, out_shape)))
        return pl.pallas_call(
            body,
            in_specs=in_specs,
            out_shape=out_shape,
            out_specs=out_specs,
            scratch_shapes=scratch,
            name=name,
            cost_estimate=pl.CostEstimate(
                flops=flops, bytes_accessed=moved, transcendentals=0
            ),
            compiler_params=pltpu.CompilerParams(
                vmem_limit_bytes=limit or min(moved + moved // 4 + 2 * MIB, 56 * MIB)
            ),
        )(*operands)

    return run


def struct(shape, dtype):
    return jax.ShapeDtypeStruct(shape, dtype)


def aligned(index, size):
    return pl.ds(pl.multiple_of(index * size, size), size)


def dot(a, b):
    return jnp.dot(a, b, preferred_element_type=F32)


def butterfly_sum(terms):
    while len(terms) > 1:
        terms = [terms[i] + terms[i + 1] for i in range(0, len(terms), 2)]
    return terms[0]


def split_rows(row):
    high = row.astype(BF16)
    low = (row - high.astype(F32)).astype(BF16)
    place = lax.broadcasted_iota(jnp.int32, (PAD, row.shape[1]), 0)
    spread = jnp.where(place == 0, high.astype(F32), 0.0)
    spread = jnp.where(place == 1, low.astype(F32), spread)
    return spread.astype(BF16)


def join_rows(rows):
    return jnp.sum(rows.astype(F32), axis=0, keepdims=True)


def split_halves(row):
    lanes = row.shape[1] // 2
    high = row.astype(BF16).astype(F32)
    low = row - high
    place = lax.broadcasted_iota(jnp.int32, (PAD, lanes), 0)
    spread = jnp.zeros((PAD, lanes), F32)
    for i, part in enumerate((high[:, :lanes], high[:, lanes:], low[:, :lanes], low[:, lanes:])):
        spread = jnp.where(place == i, part, spread)
    return spread.astype(BF16)


def join_halves(rows):
    rows = rows.astype(F32)
    place = lax.broadcasted_iota(jnp.int32, rows.shape, 0)
    left = jnp.sum(jnp.where(place % 2 == 0, rows, 0.0), axis=0, keepdims=True)
    right = jnp.sum(jnp.where(place % 2 == 1, rows, 0.0), axis=0, keepdims=True)
    return jnp.concatenate([left, right], axis=1)


def put(message, start, block):
    rows = (message.shape[0] - PAD) // 2
    count, lanes = block.shape[0], message.shape[1]
    message[start : start + count] = block[:, :lanes]
    message[rows + start : rows + start + count] = block[:, lanes:]


def flipped(k, zs):
    return k // (zs // 2)


def swap(array, axis, size, distance):
    return lax.ppermute(array, axis, [(i, i ^ distance) for i in range(size)])


def pick_kernel(requests_in, feats, keep, send, held, requests, sem):
    copy = pltpu.make_async_copy(feats, held, sem)
    copy.start()
    pltpu.sync_copy(requests_in, requests)
    copy.wait()
    blk = lax.axis_index("blk")
    for k in range(keep.shape[0]):
        flip = flipped(k, keep.shape[0])
        keep[k] = held[requests[0, blk ^ (2 * k + flip)]]
        send[k] = held[requests[0, blk ^ (2 * k + 1 - flip)]]


def join_kernel(keep, got, *messages):
    for k, message in enumerate(messages):
        flip = flipped(k, len(messages))
        message[flip] = keep[k]
        message[1 - flip] = got[k]


def prepare_kernel(
    owners, dest, slot, tiles, feats, w_self, w_neigh, cotangent, packed, rows, sem
):
    tile_count, quarter, width = tiles.shape[1:]
    row_count = packed.shape[1]
    features = w_self.shape[0]
    per_slab = row_count // width
    slabs = owners // per_slab
    rep, blk = lax.axis_index("rep"), lax.axis_index("blk")
    copy = pltpu.make_async_copy(feats.at[:, aligned(rep, quarter), :], rows, sem)
    copy.start()
    packed[:slabs] = jnp.zeros((slabs, row_count, row_count), packed.dtype)

    def place(t, carry):
        owner = slot[0, t] ^ blk
        packed[
            owner // per_slab, aligned(dest[0, t], quarter), aligned(owner % per_slab, width)
        ] = tiles[0, t]
        return carry

    lax.fori_loop(0, tile_count, place, 0)

    def turn(slab, carry):
        packed[slabs + slab] = packed[slab].T
        return carry

    lax.fori_loop(0, slabs, turn, 0)
    copy.wait()
    own = rows[...].reshape(row_count, features)
    packed[2 * slabs, :, :features] = own
    packed[2 * slabs, :, features:] = cotangent[...].reshape(row_count, features)
    packed[2 * slabs + 1, :features] = own.T
    packed[2 * slabs + 1, features:, :features] = w_self[...]
    packed[2 * slabs + 1, features:, features:] = w_neigh[...]


def layer_kernel(grad_scale, packed, bias, *refs):
    arrived, (preact_out, grad_pre_out, keep, send) = refs[:-4], refs[-4:]
    row_count, features = preact_out.shape
    zs = len(arrived)
    width = arrived[0].shape[1]
    pair = 2 * width
    per_slab = row_count // pair
    slabs = zs // per_slab
    rows = packed[2 * slabs, :, :features]
    cotangent = packed[2 * slabs, :, features:]
    rows_t = packed[2 * slabs + 1, :features]
    w_self = packed[2 * slabs + 1, features:, :features]
    w_neigh = packed[2 * slabs + 1, features:, features:]
    half = row_count // 2

    def gather_rows(part):
        total = jnp.zeros((half, features), F32)
        for k, message in enumerate(arrived):
            lanes = slice(k % per_slab * pair, (k % per_slab + 1) * pair)
            total += dot(packed[k // per_slab, part, lanes], message[...].reshape(pair, features))
        return total.astype(BF16)

    agg = jnp.concatenate([gather_rows(slice(0, half)), gather_rows(slice(half, row_count))])
    preact = dot(rows, w_self) + bias[...] + dot(agg, w_neigh)
    preact_out[...] = preact
    gating = jax.nn.sigmoid(preact)
    grad_pre = (
        cotangent.astype(F32) * gating * (1.0 + preact * (1.0 - gating))
    ).astype(BF16)
    grad_pre_out[...] = grad_pre
    back = lax.dot_general(grad_pre, w_neigh, NT, preferred_element_type=F32).astype(BF16)

    def contribute(slab, carry):
        block = dot(packed[slabs + slab], back).astype(BF16)
        for i in range(per_slab):
            place = aligned(slab * per_slab + i, width)
            keep[place, :] = block[i * pair : i * pair + width]
            send[place, :] = block[i * pair + width : (i + 1) * pair]
        return carry

    lax.fori_loop(0, slabs, contribute, 0, unroll=slabs <= 4)
    base = zs * width
    grad_self = (dot(rows_t, grad_pre) * grad_scale).astype(BF16)
    grad_neigh = (dot(agg.T, grad_pre) * grad_scale).astype(BF16)
    bias_rows = split_rows(
        jnp.sum(grad_pre.astype(F32), axis=0, keepdims=True) * grad_scale
    )
    core = lax.axis_index("blk") % 2
    for side, to_self, to_neigh in ((0, keep, send), (1, send, keep)):

        @pl.when(core == side)
        def _():
            to_self[base : base + features] = grad_self
            to_neigh[base : base + features] = grad_neigh

    keep[base + features :] = bias_rows
    send[base + features :] = bias_rows


def own_kernel(preact, grad_pre, w_self, hidden, self_term):
    value = preact[...]
    hidden[...] = (value * jax.nn.sigmoid(value)).astype(BF16).reshape(hidden.shape)
    self_term[...] = lax.dot_general(grad_pre[...], w_self[...], NT, preferred_element_type=F32)


def assemble_kernel(zs, keep, got, *refs):
    messages, gradients = refs[:-1], refs[-1]
    replicas = len(messages)
    features = keep.shape[1]
    base = keep.shape[0] - PAD - features
    width = base // zs
    quarter, share = width // replicas, features // replicas
    end = 2 * zs * quarter
    rep = lax.axis_index("rep")
    grads = slice(base, base + features)
    gradients[...] = (keep[grads].astype(F32) + got[grads].astype(F32)).astype(BF16)
    bias_rows = split_halves(
        join_rows(keep[base + features :]) + join_rows(got[base + features :])
    )
    for k, message in enumerate(messages):
        target = rep ^ k
        for z in range(zs):
            place = pl.ds(pl.multiple_of(z * width + target * quarter, quarter), quarter)
            start = 2 * z * quarter
            put(message, start, keep[place, :])
            put(message, start + quarter, got[place, :])
        put(message, end, gradients[aligned(target, share), :])
        message[2 * (end + share) :] = bias_rows


def rep_sum_kernel(zs, *refs):
    arrived, parcels = refs[:-zs], refs[-zs:]
    taken, given = (arrived[0].shape[0] - PAD) // 2, (parcels[0].shape[0] - PAD) // 2
    rows = (taken - given) // (zs - 1)
    bias_rows = split_halves(butterfly_sum([join_halves(a[2 * taken :]) for a in arrived]))
    for side in range(2):
        grads = slice(side * taken + zs * rows, (side + 1) * taken)
        grads = sum(a[grads].astype(F32) for a in arrived).astype(BF16)
        for k, parcel in enumerate(parcels):
            place = slice(side * taken + k * rows, side * taken + (k + 1) * rows)
            start = side * given
            parcel[start : start + rows] = sum(a[place].astype(F32) for a in arrived).astype(BF16)
            parcel[start + rows : start + given] = grads
    for parcel in parcels:
        parcel[2 * given :] = bias_rows


def piece_kernel(*refs):
    arrived, piece = refs[:-1], refs[-1]
    share, lanes = piece.shape[0], arrived[0].shape[1]
    given = (arrived[0].shape[0] - PAD) // 2
    for side in range(2):
        place = slice((side + 1) * given - share, (side + 1) * given)
        total = butterfly_sum([a[place].astype(F32) for a in arrived])
        piece[:, side * lanes : (side + 1) * lanes] = total.astype(BF16)


def finish_kernel(requests_in, self_term, *refs):
    arrived, (feat_grad, grad_bias, total, requests) = refs[:-4], refs[-4:]
    pltpu.sync_copy(requests_in, requests)
    grad_bias[...] = butterfly_sum([join_halves(a[a.shape[0] - PAD :]) for a in arrived])
    quarter, lanes = total.shape[1], arrived[0].shape[1]
    given = (arrived[0].shape[0] - PAD) // 2
    blk = lax.axis_index("blk")
    total[...] = self_term[...].reshape(total.shape)
    for k, message in enumerate(arrived):
        for other in range(2):
            block = requests[0, blk ^ (2 * k + other)]
            for side in range(2):
                start = side * given + other * quarter
                part = message[start : start + quarter].astype(F32)
                total[block, :, side * lanes : (side + 1) * lanes] += part
    feat_grad[...] = total[...].astype(BF16)


def gather_kernel(*refs):
    pieces, out = refs[:-1], refs[-1]
    share = pieces[0].shape[0]
    rep = lax.axis_index("rep")
    for k, piece in enumerate(pieces):
        out[aligned(rep ^ k, share), :] = piece[...]


def widen_kernel(mine, other, grad_self, grad_neigh, held, sems):
    first = lax.axis_index("blk") % 2 == 0
    a, b = mine[...], other[...]
    copies = []
    for i, (out, like, unlike) in enumerate(((grad_self, a, b), (grad_neigh, b, a))):
        held[i] = jnp.where(first, like, unlike).astype(F32)
        copies.append(pltpu.make_async_copy(held.at[i], out, sems.at[i]))
        copies[i].start()
    for copy in copies:
        copy.wait()


def on_device(feats, requests, tile_dest, tile_slot, tile_vals, w_self, w_neigh, bias, cotangent):
    owners = lax.axis_size("blk")
    replicas = lax.axis_size("rep")
    zs = owners // 2
    blk_dev, width, features = feats.shape
    quarter = width // replicas
    row_count = blk_dev * quarter
    share = features // replicas
    grad_scale = 1.0 / math.sqrt(owners * blk_dev * width)

    blocks = struct((zs, width, features), BF16)
    keep, send = call(
        pick_kernel,
        [HBM, HBM],
        (blocks, blocks),
        (VMEM, VMEM),
        (
            pltpu.VMEM(feats.shape, BF16),
            pltpu.SMEM((1, owners), jnp.int32),
            pltpu.SemaphoreType.DMA,
        ),
        name="pick",
        limit=53 * MIB,
    )(requests, feats)
    got = swap(send, "blk", owners, 1)
    messages = call(
        join_kernel,
        [VMEM, VMEM],
        (struct((2, width, features), BF16),) * zs,
        (VMEM,) * zs,
        name="join",
    )(keep, got)
    sources = [messages[0]] + [
        swap(messages[k], "blk", owners, 2 * k + flipped(k, zs)) for k in range(1, zs)
    ]
    per_slab = row_count // width
    packed = call(
        lambda *refs: prepare_kernel(owners, *refs),
        [SMEM, SMEM, VMEM, HBM, VMEM, VMEM, VMEM],
        struct((2 * (owners // per_slab) + 2, row_count, row_count), BF16),
        VMEM,
        (pltpu.VMEM((blk_dev, quarter, features), BF16), pltpu.SemaphoreType.DMA),
        name="prepare",
    )(tile_dest, tile_slot, tile_vals, feats, w_self, w_neigh, cotangent)

    sources[-1], packed = lax.optimization_barrier((sources[-1], packed))
    half = struct((zs * width + features + PAD, features), BF16)
    preact, grad_pre, keep, send = call(
        lambda *refs: layer_kernel(grad_scale, *refs),
        [VMEM] * (2 + zs),
        (struct((row_count, features), F32), struct((row_count, features), BF16), half, half),
        (VMEM,) * 4,
        name="layer",
        flops=4 * row_count * features * owners * width,
    )(packed, bias.reshape(1, features), *sources)
    got = swap(send, "blk", owners, 1)
    messages = call(
        lambda *refs: assemble_kernel(zs, *refs),
        [VMEM, VMEM],
        (struct((2 * (2 * zs * quarter + share) + PAD, features // 2), BF16),) * replicas,
        (VMEM,) * replicas,
        (pltpu.VMEM((features, features), BF16),),
        name="assemble",
    )(keep, got)
    hidden, self_term = call(
        own_kernel,
        [VMEM] * 3,
        (struct((blk_dev, quarter, features), BF16), struct((row_count, features), F32)),
        (VMEM, VMEM),
        name="own",
        flops=2 * row_count * features * features,
    )(preact, grad_pre, w_self)
    arrived = [messages[0]] + [
        swap(messages[k], "rep", replicas, k) for k in range(1, replicas)
    ]
    *arrived, self_term = lax.optimization_barrier((*arrived, self_term))
    parcels = call(
        lambda *refs: rep_sum_kernel(zs, *refs),
        [VMEM] * replicas,
        (struct((2 * (2 * quarter + share) + PAD, features // 2), BF16),) * zs,
        (VMEM,) * zs,
        name="rep_sum",
    )(*arrived)
    landed = [parcels[0]] + [swap(parcels[k], "blk", owners, 2 * k) for k in range(1, zs)]
    landed[-1], hidden = lax.optimization_barrier((landed[-1], hidden))
    piece = call(
        piece_kernel, [VMEM] * zs, struct((share, features), BF16), VMEM, name="piece"
    )(*landed)
    feat_grad, grad_bias = call(
        finish_kernel,
        [HBM, VMEM] + [VMEM] * zs,
        (struct((blk_dev, quarter, features), BF16), struct((1, features), F32)),
        (VMEM, VMEM),
        (
            pltpu.VMEM((blk_dev, quarter, features), F32),
            pltpu.SMEM((1, owners), jnp.int32),
        ),
        name="finish",
    )(requests, self_term, *landed)
    pieces = [piece] + [swap(piece, "rep", replicas, k) for k in range(1, replicas)]
    *pieces, feat_grad = lax.optimization_barrier((*pieces, feat_grad))
    whole = struct((features, features), F32)
    mine = call(
        gather_kernel,
        [VMEM] * replicas,
        struct((features, features), BF16),
        VMEM,
        name="gather_pieces",
    )(*pieces)
    other = swap(mine, "blk", owners, 1)
    other, feat_grad = lax.optimization_barrier((other, feat_grad))
    grad_self, grad_neigh = call(
        widen_kernel,
        [VMEM, VMEM],
        (whole, whole),
        (HBM, HBM),
        (pltpu.VMEM((2, features, features), F32), pltpu.SemaphoreType.DMA((2,))),
        name="widen",
    )(mine, other)
    return (hidden, grad_self, grad_neigh, grad_bias.reshape(features), feat_grad)


def solution(mesh):
    in_specs = (
        P("blk", None, None),
        P("blk", None),
        P("blk", None),
        P("blk", None),
        P("blk", None, "rep", None),
        P(),
        P(),
        P(),
        P("blk", "rep", None),
    )
    out_specs = (P("blk", "rep", None), P(), P(), P(), P("blk", "rep", None))
    return jax.shard_map(
        on_device, mesh=mesh, in_specs=in_specs, out_specs=out_specs, check_vma=False
    )
```
